32 devices in a mesh: ctx: 8 (over z, x), dp: 4 (over y, core).
Axes of the slice: x: 2, y: 2, z: 4, core: 2. Of those that a mesh axis runs over, the one named last changes fastest.
Arguments:
- inner_input: bfloat16 [24576, 4096], P(('dp', 'ctx')), parts along dimension 0, may hold values from -6 to 6
- state_proj: bfloat16 [24576, 256], P(('dp', 'ctx')), parts along dimension 0, may hold values from -6 to 6
- step_size: float32 [24576, 64], P(('dp', 'ctx')), parts along dimension 0, may hold values from 0.004 to 0.04
- decay_log: float32 [24576, 64], P(('dp', 'ctx')), parts along dimension 0, may hold values from -1 to 0
- conv_inner: float32 [4, 4096], replicated, may hold values from -3 to 3
- conv_proj: float32 [4, 256], replicated, may hold values from -3 to 3
- skip_weight: float32 [64], replicated, may hold values from 0.5 to 2.5
- norm_gain: float32 [4096], replicated, may hold values from 0.5 to 1.5
Outputs:
- layer_output: bfloat16 [24576, 4096], P(('dp', 'ctx')), parts along dimension 0
The draws below stay inside these ranges and needn't reach their ends.
There are 4 independent parts, one for each index of `dp`. The reference program is written for one: setup_inputs(seed, part) draws one part's arguments, and reference() takes and returns one part's arrays. A program takes and returns all parts, laid end to end along the dimension named above; an argument that names none is the same for every part. Nothing has to cross between parts.
All inputs are finite; a program needn't handle non-finite values.
Results may differ from the reference program's by a relative error of at most 0.0045.
Values may be sent and summed in bfloat16 or wider, within the bound.
No kernel may reach another device: no remote copies, remote signals or barrier semaphores. Data moves between devices by JAX's collectives and lax.ppermute only.
A program may use at most 192 MiB of HBM per device.

```python
import math
import jax
import jax.numpy as jnp
from jax import lax

HEAD_GROUP = 64
HEAD_DIM = 64
STATE = 128
BLOCK = 256
KERNEL = 4
SEQUENCE_TOKENS = 6144


def draw_decay_log(key, part):
    key = jax.random.fold_in(key, 11)
    random_keys = jax.random.split(key, 7)
    slow_share = 0.5
    slow_heads = jax.random.uniform(random_keys[0], (HEAD_GROUP,)) < slow_share
    slow_rate = jax.random.uniform(random_keys[1], (HEAD_GROUP,), minval=0.2, maxval=0.6) / SEQUENCE_TOKENS
    fast_rate = jnp.exp(jax.random.uniform(random_keys[2], (HEAD_GROUP,), minval=math.log(1.0 / 50.0), maxval=math.log(1.0 / 25.0)))
    head_rate = jnp.where(slow_heads, slow_rate, fast_rate)
    token_factor = jnp.exp(jax.random.uniform(random_keys[3], (SEQUENCE_TOKENS // BLOCK, BLOCK, HEAD_GROUP), minval=-0.7, maxval=0.7))
    block_factor = jnp.exp(jax.random.uniform(random_keys[4], (SEQUENCE_TOKENS // BLOCK, 1, HEAD_GROUP), minval=-0.7, maxval=0.7))
    baseline_decay_rate = (token_factor * block_factor).reshape(SEQUENCE_TOKENS, HEAD_GROUP) * head_rate[None, :]
    spike_positions = jax.random.randint(random_keys[5], (4,), 0, SEQUENCE_TOKENS)
    spike_token_rows = jnp.any(jnp.arange(SEQUENCE_TOKENS)[:, None] == spike_positions[None, :], axis=1)
    spike_loss_value = jax.random.uniform(random_keys[6], (SEQUENCE_TOKENS, HEAD_GROUP), minval=0.22, maxval=0.69)
    return -(baseline_decay_rate + jnp.where(spike_token_rows[:, None], spike_loss_value, 0.0))


def levels(rng, extent, shards, smallest, largest):
    factor_of = 1.0
    for axis_at, blocks in shards:
        steps = jax.random.uniform(jax.random.fold_in(jax.random.fold_in(rng, 6), axis_at), (blocks,), jnp.float32, smallest / len(shards), largest / len(shards))
        factor_of = factor_of * jnp.repeat(jnp.exp(steps), extent[axis_at] // blocks).reshape((-1,) + (1,) * (len(extent) - 1 - axis_at))
    return factor_of


def normal_values(rng, dims, scale, most, shards=(), dtype=jnp.bfloat16):
    drawn = scale * jax.random.normal(rng, dims, jnp.float32)
    if shards:
        drawn = drawn * levels(rng, dims, shards, -0.22, 0.18)
    return jnp.clip(drawn, -most, most).astype(dtype)


def setup_inputs(seed: int = 0, part: int = 0) -> dict:
    streams_of = jax.random.split(jax.random.key(seed), 9)
    part_keys = jax.random.split(jax.random.fold_in(streams_of[8], part), 9)
    inner_input = normal_values(part_keys[0], (SEQUENCE_TOKENS, HEAD_GROUP * HEAD_DIM), 1.0, 6.0, ((0, 8),))
    state_proj = normal_values(part_keys[1], (SEQUENCE_TOKENS, 2 * STATE), 1.0, 6.0, ((0, 8),))
    step_size = jnp.clip(jnp.exp(math.log(0.04) - 2.30258502 * jax.random.uniform(part_keys[2], (SEQUENCE_TOKENS, HEAD_GROUP), jnp.float32) ** levels(part_keys[2], (SEQUENCE_TOKENS, HEAD_GROUP), ((0, 8),), -0.2, 0.2)), 0.004, 0.04)
    decay_log = draw_decay_log(jax.random.fold_in(jax.random.fold_in(streams_of[8], part), 71), part)
    conv_inner = normal_values(streams_of[4], (KERNEL, HEAD_GROUP * HEAD_DIM), KERNEL ** -0.5, 3.0, (), jnp.float32)
    conv_proj = normal_values(streams_of[5], (KERNEL, 2 * STATE), KERNEL ** -0.5, 3.0, (), jnp.float32)
    skip_weight = jnp.clip(jax.random.uniform(streams_of[6], (HEAD_GROUP,), jnp.float32, 0.5, 2.5), 0.5, 2.5)
    norm_gain = jnp.clip(1.0 + 0.1 * jax.random.normal(streams_of[7], (HEAD_GROUP * HEAD_DIM,), jnp.float32), 0.5, 1.5)
    return {"inner_input": inner_input, "state_proj": state_proj, "step_size": step_size, "decay_log": decay_log, "conv_inner": conv_inner, "conv_proj": conv_proj, "skip_weight": skip_weight, "norm_gain": norm_gain}


def silu_conv(window, weights, length):
    summed = jnp.zeros((length, weights.shape[1]), jnp.float32)
    for offset in range(weights.shape[0]):
        summed = summed + window[offset:offset + length].astype(jnp.float32) * weights[offset]
    return jax.nn.silu(summed).astype(jnp.bfloat16)

def block_terms(inner_rows, project, step_block, decays):
    length = inner_rows.shape[0]
    state_width = project.shape[1] // 2
    b_rows = project[:, :state_width]
    c_rows = project[:, state_width:]
    cumulative = jnp.cumsum(decays, axis=0)
    scores = jnp.dot(c_rows, b_rows.T, preferred_element_type=jnp.float32)
    positions = jnp.arange(length)
    causal = positions[:, None] >= positions[None, :]
    spread = cumulative.T[:, :, None] - cumulative.T[:, None, :]
    decay_table = jnp.where(causal[None], jnp.exp(jnp.minimum(spread, 0.0)), 0.0)
    weights = (scores[None] * decay_table * step_block.T[:, None, :]).astype(jnp.bfloat16)
    inside = jnp.einsum('hts,shp->thp', weights.astype(jnp.float32), inner_rows.astype(jnp.float32))
    totals = cumulative[-1]
    scaled = ((jnp.exp(totals[None, :] - cumulative) * step_block)[:, :, None] * inner_rows.astype(jnp.float32)).astype(jnp.bfloat16)
    block_state = jnp.einsum('shp,sn->hpn', scaled.astype(jnp.float32), b_rows.astype(jnp.float32))
    return (inside, block_state, cumulative, totals, c_rows)

def reference(inner_input, state_proj, step_size, decay_log, conv_inner, conv_proj, skip_weight, norm_gain):
    pad_rows = KERNEL - 1
    inner_pad = jnp.pad(inner_input, ((pad_rows, 0), (0, 0)))
    proj_pad = jnp.pad(state_proj, ((pad_rows, 0), (0, 0)))
    gain_table = norm_gain.reshape(HEAD_GROUP, HEAD_DIM)

    def advance(incoming, block_index):
        first_row = (block_index * BLOCK).astype(jnp.int32)
        inner_rows = silu_conv(lax.dynamic_slice_in_dim(inner_pad, first_row, BLOCK + pad_rows, 0), conv_inner, BLOCK)
        project = silu_conv(lax.dynamic_slice_in_dim(proj_pad, first_row, BLOCK + pad_rows, 0), conv_proj, BLOCK)
        step_block = lax.dynamic_slice_in_dim(step_size, first_row, BLOCK, 0)
        decays = lax.dynamic_slice_in_dim(decay_log, first_row, BLOCK, 0)
        inner_heads = inner_rows.reshape(BLOCK, HEAD_GROUP, HEAD_DIM)
        inside, block_state, cumulative, totals, c_rows = block_terms(inner_heads, project, step_block, decays)
        entering_b = incoming.astype(jnp.bfloat16)
        carried_part = jnp.einsum('tn,hpn->thp', c_rows.astype(jnp.float32), entering_b.astype(jnp.float32))
        combined = inside + jnp.exp(cumulative)[:, :, None] * carried_part + skip_weight[None, :, None] * inner_heads.astype(jnp.float32)
        inverse_rms = lax.rsqrt(lax.optimization_barrier(jnp.mean(combined * combined, axis=2, keepdims=True)) + 1e-05)
        result = (combined * inverse_rms * gain_table[None]).astype(jnp.bfloat16).reshape(BLOCK, HEAD_GROUP * HEAD_DIM)
        following = jnp.exp(totals)[:, None, None] * incoming + block_state
        return (following, result)
    opening = jnp.zeros((HEAD_GROUP, HEAD_DIM, STATE), jnp.float32)
    final_state, outputs = lax.scan(advance, opening, jnp.arange(SEQUENCE_TOKENS // BLOCK))
    return outputs.reshape(SEQUENCE_TOKENS, HEAD_GROUP * HEAD_DIM)
```

```python
import jax
import jax.numpy as jnp
from jax import lax
from jax.experimental import pallas as pl
from jax.experimental.pallas import tpu as pltpu
from jax.sharding import PartitionSpec as P

CHUNK = 128
SQUARE = 4
GROUPS = 2
SUB = 256
EDGE = 16
F32 = jnp.float32
BF16 = jnp.bfloat16


def params(mib=16):
    return pltpu.CompilerParams(vmem_limit_bytes=mib * 1024 * 1024)


def dot(a, b):
    return jnp.dot(a, b, preferred_element_type=F32)


def exact_dot(a, b):
    return jnp.dot(a, b, preferred_element_type=F32, precision=lax.Precision.HIGHEST)


def iota(shape, axis):
    return lax.broadcasted_iota(jnp.int32, shape, axis)


def hi_lo(value):
    half = value.shape[1] // 2
    high = value.astype(BF16).astype(F32)
    return jnp.where(iota(value.shape, 1) < half, high, value - high).astype(BF16)


def spread(heads, head_width, first, cols):
    row = iota((2 * heads, cols), 0)
    row = jnp.where(row >= heads, row - heads, row)
    col = first + iota((2 * heads, cols), 1)
    low = row * head_width
    return jnp.where((col >= low) & (col < low + head_width), 1.0, 0.0).astype(BF16)


def silu_conv(window, half_taps):
    taps = len(half_taps)
    summed = window[8:] * half_taps[taps - 1]
    for back in range(1, taps):
        summed = summed + pltpu.roll(window, back, 0)[8:] * half_taps[taps - 1 - back]
    return (summed + summed * jnp.tanh(summed)).astype(BF16)


def decay_kernel(decay_ref, step_ref, skip_ref, fwd_ref, inv_ref, dev_ref, end_ref, fac_ref, total_ref):
    rows, heads = decay_ref.shape
    chunks = rows // CHUNK
    twice = jnp.where(iota((heads, 2 * heads), 0) == iota((heads, 2 * heads), 1) % heads, 1.0, 0.0)
    lower = jnp.where(iota((CHUNK, CHUNK), 0) >= iota((CHUNK, CHUNK), 1), 1.0, 0.0)
    cums, steps = [], []
    for c in range(chunks):
        at = pl.ds(c * CHUNK, CHUNK)
        cums.append(exact_dot(lower, exact_dot(decay_ref[at, :], twice)))
        steps.append(exact_dot(step_ref[at, :], twice))
    totals = [cum[CHUNK - 1 :] for cum in cums]
    middles = [cum[CHUNK // 2 - 1 : CHUNK // 2] for cum in cums]
    before = [jnp.zeros_like(totals[0])]
    for c in range(chunks):
        before.append(before[c] + totals[c])
    after = [jnp.zeros_like(totals[0])]
    for c in range(chunks - 1, 0, -1):
        after.insert(0, after[0] + totals[c])
    fac_rows = []
    for c in range(chunks):
        at = pl.ds(c * CHUNK, CHUNK)
        fwd_ref[at, :] = hi_lo(jnp.exp(cums[c] - middles[c]))
        inv_ref[at, :] = hi_lo(jnp.exp(middles[c] - cums[c]) * steps[c])
        dev_ref[at, :] = hi_lo(jnp.exp(before[c] + cums[c]))
        end_ref[at, :] = hi_lo(jnp.exp((totals[c] - cums[c]) + after[c]) * steps[c])
        following = middles[c + 1] if c + 1 < chunks else 0.0
        fac_rows.append(jnp.exp(totals[c] - middles[c] + following))
    skip = exact_dot(skip_ref[...], twice)
    row = iota((16, 2 * heads), 0)
    fac = jnp.where(row == chunks, skip[:1], 0.0)
    for c in range(chunks):
        fac = jnp.where(row == c, fac_rows[c], fac)
    fac_ref[...] = hi_lo(fac)
    total_ref[...] = jnp.broadcast_to(before[chunks], total_ref.shape)


def decays(decay_log, step_size, skip_weight):
    rows, heads = decay_log.shape
    wide = jax.ShapeDtypeStruct((rows, 2 * heads), BF16)
    return pl.pallas_call(
        decay_kernel,
        out_shape=(wide, wide, wide, wide, jax.ShapeDtypeStruct((16, 2 * heads), BF16), jax.ShapeDtypeStruct((8, 2 * heads), F32)),
        compiler_params=params(),
        name="decays",
    )(decay_log, step_size, jnp.broadcast_to(skip_weight[None], (8, heads)))


def chunk_window(ref, edge_ref, c, cols):
    if c == 0:
        past = edge_ref[:, cols].astype(F32)[EDGE - 8 :]
    else:
        past = ref[pl.ds(c * CHUNK - EDGE, EDGE), cols].astype(F32)[EDGE - 8 :]
    return jnp.concatenate([past, ref[pl.ds(c * CHUNK, CHUNK), cols].astype(F32)], axis=0)


def proj_kernel(proj_ref, edge_ref, taps_ref, mix_ref, bt_ref):
    rows, width = proj_ref.shape
    state = width // 2
    taps = [0.5 * taps_ref[k : k + 1, :] for k in range(taps_ref.shape[0])]
    causal = iota((CHUNK, CHUNK), 0) >= iota((CHUNK, CHUNK), 1)
    for c in range(rows // CHUNK):
        at = pl.ds(c * CHUNK, CHUNK)
        both = silu_conv(chunk_window(proj_ref, edge_ref, c, slice(None)), taps)
        b_rows, c_rows = both[:, :state], both[:, state:]
        b_cols = b_rows.astype(F32).T.astype(BF16)
        scores = dot(c_rows, b_cols)
        mix_ref[at, :CHUNK] = jnp.where(causal, scores, 0.0).astype(BF16)
        mix_ref[at, CHUNK:] = c_rows
        bt_ref[:, at] = b_cols


def projections(state_proj, edge, taps):
    rows, width = state_proj.shape
    state = width // 2
    return pl.pallas_call(
        proj_kernel,
        out_shape=(jax.ShapeDtypeStruct((rows, CHUNK + state), BF16), jax.ShapeDtypeStruct((state, rows), BF16)),
        compiler_params=params(),
        name="projections",
    )(state_proj, edge, taps)


def state_kernel(place_ref, in_ref, edge_ref, taps_ref, end_ref, bt_ref, x_ref, *rest, head_width, first):
    slots, scaled_ref = rest[:-1], rest[-1]
    rows, cols = in_ref.shape
    heads = end_ref.shape[1] // 2
    tile = pl.program_id(0)
    for sub in range(cols // SUB):
        at_cols = pl.ds(sub * SUB, SUB)
        table = spread(heads, head_width, first + tile * cols + sub * SUB, SUB)
        taps = [0.5 * taps_ref[k : k + 1, at_cols] for k in range(taps_ref.shape[0])]
        for c in range(rows // CHUNK):
            at = pl.ds(c * CHUNK, CHUNK)
            x = silu_conv(chunk_window(in_ref, edge_ref, c, at_cols), taps)
            x_ref[at, at_cols] = x
            scaled_ref[at, at_cols] = (dot(end_ref[at, :], table) * x.astype(F32)).astype(BF16)
    summary = dot(bt_ref[...], scaled_ref[...]).astype(BF16)
    slot = tile ^ place_ref[0]
    for k in range(len(slots)):

        @pl.when(slot == k)
        def _():
            slots[k][...] = summary


def device_states(place, inner, edge, taps, end, bt, head_width, group):
    rows, width = inner.shape
    state = bt.shape[0]
    wide = width // GROUPS
    cols = wide // SQUARE
    base = group * SQUARE
    whole = lambda a: pl.BlockSpec(a.shape, lambda j, p: (0,) * a.ndim)
    column = lambda n: pl.BlockSpec((n, cols), lambda j, p: (0, base + j))
    slot = jax.ShapeDtypeStruct((state, cols), BF16)
    out = pl.pallas_call(
        lambda *refs: state_kernel(*refs, head_width=head_width, first=group * wide),
        grid_spec=pltpu.PrefetchScalarGridSpec(
            num_scalar_prefetch=1,
            grid=(SQUARE,),
            in_specs=[column(rows), column(edge.shape[0]), column(taps.shape[0]), whole(end), whole(bt)],
            out_specs=[pl.BlockSpec((rows, cols), lambda j, p: (0, j))] + [pl.BlockSpec((state, cols), lambda j, p: (0, 0))] * SQUARE,
            scratch_shapes=[pltpu.VMEM((rows, cols), BF16)],
        ),
        out_shape=[jax.ShapeDtypeStruct((rows, wide), BF16)] + [slot] * SQUARE,
        compiler_params=params(),
        cost_estimate=pl.CostEstimate(flops=2 * rows * wide * 2 * state, bytes_accessed=4 * rows * wide, transcendentals=rows * wide),
        name="states",
    )(place, inner, edge, taps, end, bt)
    return out[0], out[1:]


def local_kernel(x_ref, fwd_ref, inv_ref, fac_ref, mix_ref, bt_ref, out_ref, both_ref, state_ref, *, head_width, first):
    rows, cols = x_ref.shape
    heads = fwd_ref.shape[1] // 2
    chunks = rows // CHUNK
    for sub in range(cols // SUB):
        at_cols = pl.ds(sub * SUB, SUB)
        table = spread(heads, head_width, first + pl.program_id(0) * cols + sub * SUB, SUB)
        factors = dot(fac_ref[...], table)
        skip = factors[chunks : chunks + 1]
        state = jnp.zeros((bt_ref.shape[0], SUB), F32)
        for c in range(chunks):
            at = pl.ds(c * CHUNK, CHUNK)
            x = x_ref[at, at_cols].astype(F32)
            scaled = (dot(inv_ref[at, :], table) * x).astype(BF16)
            both = jnp.concatenate([scaled, state.astype(BF16)], axis=0)
            mixed = dot(mix_ref[at, :], both)
            out_ref[at, at_cols] = dot(fwd_ref[at, :], table) * mixed + skip * x
            if c + 1 < chunks:
                state = factors[c : c + 1] * (state + dot(bt_ref[:, at], scaled))


def local_parts(x, fwd, inv, fac, mix, bt, head_width, group):
    rows, wide = x.shape
    cols = wide // SQUARE
    state = bt.shape[0]
    whole = lambda a: pl.BlockSpec(a.shape, lambda j: (0,) * a.ndim)
    column = pl.BlockSpec((rows, cols), lambda j: (0, j))
    return pl.pallas_call(
        lambda *refs: local_kernel(*refs, head_width=head_width, first=group * wide),
        grid=(SQUARE,),
        in_specs=[column, whole(fwd), whole(inv), whole(fac), whole(mix), whole(bt)],
        out_specs=column,
        out_shape=jax.ShapeDtypeStruct((rows, wide), F32),
        scratch_shapes=[pltpu.VMEM((CHUNK + state, SUB), BF16), pltpu.VMEM((state, SUB), F32)],
        compiler_params=params(),
        cost_estimate=pl.CostEstimate(flops=2 * rows * wide * 5 * state, bytes_accessed=6 * rows * wide, transcendentals=0),
        name="local",
    )(x, fwd, inv, fac, mix, bt)


def final_kernel(place_ref, local_ref, dev_ref, mix_ref, gain_ref, *rest, head_width, first):
    slots, out_ref, state_ref = rest[:-2], rest[-2], rest[-1]
    rows, cols = local_ref.shape
    heads = dev_ref.shape[1] // 2
    step = pl.program_id(0)
    tile = step ^ place_ref[0]
    for k in range(len(slots)):

        @pl.when(step == k)
        def _():
            state_ref[...] = slots[k][...]

    mean = jnp.where(iota((SUB, SUB), 0) // head_width == iota((SUB, SUB), 1) // head_width, 1.0 / head_width, 0.0).astype(BF16)
    for sub in range(cols // SUB):
        at_cols = pl.ds(sub * SUB, SUB)
        table = spread(heads, head_width, first + tile * cols + sub * SUB, SUB)
        gain = gain_ref[:, at_cols]
        for c in range(rows // CHUNK):
            at = pl.ds(c * CHUNK, CHUNK)
            carried = dot(mix_ref[at, CHUNK:], state_ref[:, at_cols])
            combined = local_ref[at, at_cols] + dot(dev_ref[at, :], table) * carried
            squares = dot((combined * combined).astype(BF16), mean)
            out_ref[at, at_cols] = (combined * lax.rsqrt(squares + 1e-05) * gain).astype(BF16)


def finish(place, local, dev, mix, gain, slots, head_width, group, into):
    rows, wide = local.shape
    cols = wide // SQUARE
    base = group * SQUARE
    whole = lambda a: pl.BlockSpec(a.shape, lambda k, p: (0,) * a.ndim)
    in_specs = [
        pl.BlockSpec((rows, cols), lambda k, p: (0, k ^ p[0])),
        whole(dev),
        whole(mix),
        pl.BlockSpec((1, cols), lambda k, p: (0, base + (k ^ p[0]))),
    ] + [whole(s) for s in slots]
    operands = [place, local, dev, mix, gain, *slots]
    aliases = {}
    if into is not None:
        in_specs.append(pl.BlockSpec(memory_space=pl.ANY))
        operands.append(into)
        aliases = {len(operands) - 1: 0}

    def kernel(*refs):
        count = 5 + len(slots)
        skipped = 0 if into is None else 1
        final_kernel(*refs[:count], *refs[count + skipped :], head_width=head_width, first=group * wide)

    return pl.pallas_call(
        kernel,
        grid_spec=pltpu.PrefetchScalarGridSpec(
            num_scalar_prefetch=1,
            grid=(SQUARE,),
            in_specs=in_specs,
            out_specs=pl.BlockSpec((rows, cols), lambda k, p: (0, base + (k ^ p[0]))),
            scratch_shapes=[pltpu.VMEM(slots[0].shape, BF16)],
        ),
        out_shape=jax.ShapeDtypeStruct((rows, wide * GROUPS), BF16),
        input_output_aliases=aliases,
        compiler_params=params(),
        cost_estimate=pl.CostEstimate(flops=2 * rows * wide * 512, bytes_accessed=6 * rows * wide, transcendentals=rows * wide),
        name="finish",
    )(*operands)


def shifted(x, by):
    length = lax.axis_size("ctx")
    return lax.ppermute(x, "ctx", [(i, i + by) for i in range(length - by)])


def swapped(x, k):
    length = lax.axis_size("ctx")
    return lax.ppermute(x, "ctx", [(i, i ^ k) for i in range(length)])


def per_column(weights, head_width):
    return jnp.repeat(weights, head_width, axis=-1)


def square_weights(totals, place):
    position = jnp.arange(SQUARE) ^ place
    between = lambda low, high: jnp.sum(jnp.where(((position > low) & (position < high))[:, None], totals, 0.0), axis=0)
    ends = [position[k] for k in range(SQUARE)] + [SQUARE]
    inner = jnp.stack([
        jnp.stack([jnp.where(position[q] < ends[k], jnp.exp(between(position[q], ends[k])), 0.0) for q in range(SQUARE)])
        for k in range(SQUARE + 1)
    ])
    opening = jnp.stack([jnp.exp(between(-1, ends[k])) for k in range(SQUARE)])
    return inner, opening, jnp.sum(totals, axis=0)


def previous_squares(leaving, total, head_width):
    squares = lax.axis_size("ctx") // SQUARE
    entering = shifted(leaving, SQUARE)
    span = 1
    if squares > 2:
        window = shifted(total, SQUARE)
    while span < squares - 1:
        behind = shifted(entering, SQUARE * span)
        entering = entering.astype(F32) + per_column(jnp.exp(window), head_width) * behind.astype(F32)
        entering = entering.astype(BF16)
        window = window + shifted(window, SQUARE * span)
        span *= 2
    return entering


def body(inner_input, state_proj, step_size, decay_log, conv_inner, conv_proj, skip_weight, norm_gain):
    rows, width = inner_input.shape
    heads = step_size.shape[1]
    head_width = width // heads
    spot = lax.axis_index("ctx") % SQUARE
    place = jnp.full((1,), spot, jnp.int32)
    edge_inner = shifted(inner_input[rows - EDGE :], 1)
    edge_proj = shifted(state_proj[rows - EDGE :], 1)
    fwd, inv, dev, end, fac, total = decays(decay_log, step_size, skip_weight)
    total = total[:1, :heads]
    totals = jnp.concatenate([total] + [swapped(total, k) for k in range(1, SQUARE)], axis=0)
    inner_weights, opening, square_total = square_weights(totals, spot)
    mix, bt = projections(state_proj, edge_proj, conv_proj)
    gain = norm_gain[None]
    wide = width // GROUPS
    xs, sent = [], []
    for group in range(GROUPS):
        x, slots = device_states(place, inner_input, edge_inner, conv_inner, end, bt, head_width, group)
        xs.append(x)
        sent.append([slots[0]] + [swapped(slots[k], k) for k in range(1, SQUARE)])
    quarter = wide // SQUARE
    quarter_heads = quarter // head_width
    returned = []
    for group in range(GROUPS):
        first = (group * SQUARE + spot) * quarter_heads
        pick = lambda w: per_column(lax.dynamic_slice_in_dim(w, first, quarter_heads, w.ndim - 1), head_width)
        weights, opened = pick(inner_weights), pick(opening)
        held = [s.astype(F32) for s in sent[group]]
        prefix = [sum(weights[k, q][None] * held[q] for q in range(SQUARE)) for k in range(SQUARE + 1)]
        leaving = prefix[SQUARE].astype(BF16)
        arrived = previous_squares(leaving, lax.dynamic_slice_in_dim(square_total, first, quarter_heads, 0), head_width).astype(F32)
        entering = [(prefix[k] + opened[k][None] * arrived).astype(BF16) for k in range(SQUARE)]
        returned.append([entering[0]] + [swapped(entering[k], k) for k in range(1, SQUARE)])
    locals_ = [local_parts(xs[g], fwd, inv, fac, mix, bt, head_width, g) for g in range(GROUPS)]
    out = None
    for group in range(GROUPS):
        out = finish(place, locals_[group], dev, mix, gain, returned[group], head_width, group, out)
    return out


def solution(mesh):
    split = P(("dp", "ctx"), None)
    return jax.shard_map(
        body, mesh=mesh, in_specs=(split, split, split, split, P(), P(), P(), P()), out_specs=split, check_vma=False
    )
```

```python
import jax
import jax.numpy as jnp
from jax import lax
from jax.experimental import pallas as pl
from jax.experimental.pallas import tpu as pltpu
from jax.sharding import PartitionSpec as P

CHUNK = 128
SQUARE = 4
GROUPS = 2
SUB = 256
EDGE = 16
F32 = jnp.float32
BF16 = jnp.bfloat16


def params(mib=16):
    return pltpu.CompilerParams(vmem_limit_bytes=mib * 1024 * 1024)


def dot(a, b):
    return jnp.dot(a, b, preferred_element_type=F32)


def exact_dot(a, b):
    return jnp.dot(a, b, preferred_element_type=F32, precision=lax.Precision.HIGHEST)


def iota(shape, axis):
    return lax.broadcasted_iota(jnp.int32, shape, axis)


def hi_lo(value):
    half = value.shape[1] // 2
    high = value.astype(BF16).astype(F32)
    return jnp.where(iota(value.shape, 1) < half, high, value - high).astype(BF16)


def spread(heads, head_width, first, cols):
    row = iota((2 * heads, cols), 0)
    row = jnp.where(row >= heads, row - heads, row)
    col = first + iota((2 * heads, cols), 1)
    low = row * head_width
    return jnp.where((col >= low) & (col < low + head_width), 1.0, 0.0).astype(BF16)


def silu_conv(window, half_taps):
    taps = len(half_taps)
    summed = window[8:] * half_taps[taps - 1]
    for back in range(1, taps):
        summed = summed + pltpu.roll(window, back, 0)[8:] * half_taps[taps - 1 - back]
    return (summed + summed * jnp.tanh(summed)).astype(BF16)


def decay_kernel(decay_ref, step_ref, skip_ref, fwd_ref, inv_ref, dev_ref, end_ref, fac_ref, total_ref):
    rows, heads = decay_ref.shape
    chunks = rows // CHUNK
    twice = jnp.where(iota((heads, 2 * heads), 0) == iota((heads, 2 * heads), 1) % heads, 1.0, 0.0)
    lower = jnp.where(iota((CHUNK, CHUNK), 0) >= iota((CHUNK, CHUNK), 1), 1.0, 0.0)
    cums, steps = [], []
    for c in range(chunks):
        at = pl.ds(c * CHUNK, CHUNK)
        cums.append(exact_dot(lower, exact_dot(decay_ref[at, :], twice)))
        steps.append(exact_dot(step_ref[at, :], twice))
    totals = [cum[CHUNK - 1 :] for cum in cums]
    middles = [cum[CHUNK // 2 - 1 : CHUNK // 2] for cum in cums]
    before = [jnp.zeros_like(totals[0])]
    for c in range(chunks):
        before.append(before[c] + totals[c])
    after = [jnp.zeros_like(totals[0])]
    for c in range(chunks - 1, 0, -1):
        after.insert(0, after[0] + totals[c])
    fac_rows = []
    for c in range(chunks):
        at = pl.ds(c * CHUNK, CHUNK)
        fwd_ref[at, :] = hi_lo(jnp.exp(cums[c] - middles[c]))
        inv_ref[at, :] = hi_lo(jnp.exp(middles[c] - cums[c]) * steps[c])
        dev_ref[at, :] = hi_lo(jnp.exp(before[c] + cums[c]))
        end_ref[at, :] = hi_lo(jnp.exp((totals[c] - cums[c]) + after[c]) * steps[c])
        following = middles[c + 1] if c + 1 < chunks else 0.0
        fac_rows.append(jnp.exp(totals[c] - middles[c] + following))
    skip = exact_dot(skip_ref[...], twice)
    row = iota((16, 2 * heads), 0)
    fac = jnp.where(row == chunks, skip[:1], 0.0)
    for c in range(chunks):
        fac = jnp.where(row == c, fac_rows[c], fac)
    fac_ref[...] = hi_lo(fac)
    total_ref[...] = jnp.broadcast_to(before[chunks], total_ref.shape)


def decays(decay_log, step_size, skip_weight):
    rows, heads = decay_log.shape
    wide = jax.ShapeDtypeStruct((rows, 2 * heads), BF16)
    return pl.pallas_call(
        decay_kernel,
        out_shape=(wide, wide, wide, wide, jax.ShapeDtypeStruct((16, 2 * heads), BF16), jax.ShapeDtypeStruct((8, 2 * heads), F32)),
        compiler_params=params(),
        name="decays",
    )(decay_log, step_size, jnp.broadcast_to(skip_weight[None], (8, heads)))


def chunk_window(ref, edge_ref, c, cols):
    if c == 0:
        past = edge_ref[:, cols].astype(F32)[EDGE - 8 :]
    else:
        past = ref[pl.ds(c * CHUNK - EDGE, EDGE), cols].astype(F32)[EDGE - 8 :]
    return jnp.concatenate([past, ref[pl.ds(c * CHUNK, CHUNK), cols].astype(F32)], axis=0)


def proj_kernel(proj_ref, edge_ref, taps_ref, mix_ref, bt_ref):
    rows, width = proj_ref.shape
    state = width // 2
    taps = [0.5 * taps_ref[k : k + 1, :] for k in range(taps_ref.shape[0])]
    causal = iota((CHUNK, CHUNK), 0) >= iota((CHUNK, CHUNK), 1)
    for c in range(rows // CHUNK):
        at = pl.ds(c * CHUNK, CHUNK)
        both = silu_conv(chunk_window(proj_ref, edge_ref, c, slice(None)), taps)
        b_rows, c_rows = both[:, :state], both[:, state:]
        b_cols = b_rows.astype(F32).T.astype(BF16)
        scores = dot(c_rows, b_cols)
        mix_ref[at, :CHUNK] = jnp.where(causal, scores, 0.0).astype(BF16)
        mix_ref[at, CHUNK:] = c_rows
        bt_ref[:, at] = b_cols


def projections(state_proj, edge, taps):
    rows, width = state_proj.shape
    state = width // 2
    whole = lambda a, b: pl.BlockSpec((a, b), lambda i: (0, 0))
    last = edge.shape[1] // width - 1
    return pl.pallas_call(
        proj_kernel,
        grid=(1,),
        in_specs=[whole(rows, width), pl.BlockSpec((EDGE, width), lambda i: (0, last)), whole(*taps.shape)],
        out_specs=(whole(rows, CHUNK + state), whole(state, rows)),
        out_shape=(jax.ShapeDtypeStruct((rows, CHUNK + state), BF16), jax.ShapeDtypeStruct((state, rows), BF16)),
        compiler_params=params(),
        name="projections",
    )(state_proj, edge, taps)


def state_kernel(place_ref, in_ref, edge_ref, taps_ref, end_ref, bt_ref, x_ref, *rest, head_width, first):
    slots, scaled_ref = rest[:-1], rest[-1]
    rows, cols = in_ref.shape
    heads = end_ref.shape[1] // 2
    tile = pl.program_id(0)
    for sub in range(cols // SUB):
        at_cols = pl.ds(sub * SUB, SUB)
        table = spread(heads, head_width, first + tile * cols + sub * SUB, SUB)
        taps = [0.5 * taps_ref[k : k + 1, at_cols] for k in range(taps_ref.shape[0])]
        for c in range(rows // CHUNK):
            at = pl.ds(c * CHUNK, CHUNK)
            x_ref[at, at_cols] = silu_conv(chunk_window(in_ref, edge_ref, c, at_cols), taps)
        scaled_ref[:, at_cols] = (dot(end_ref[...], table) * x_ref[:, at_cols].astype(F32)).astype(BF16)
    summary = dot(bt_ref[...], scaled_ref[...]).astype(BF16)
    slot = tile ^ place_ref[0]
    for k in range(len(slots)):

        @pl.when(slot == k)
        def _():
            slots[k][...] = summary


def device_states(place, inner, edge, taps, end, bt, head_width, group):
    rows, width = inner.shape
    state = bt.shape[0]
    wide = width // GROUPS
    cols = wide // SQUARE
    base = group * SQUARE
    whole = lambda a: pl.BlockSpec(a.shape, lambda j, p: (0,) * a.ndim)
    column = lambda n: pl.BlockSpec((n, cols), lambda j, p: (0, base + j))
    slot = jax.ShapeDtypeStruct((state, cols), BF16)
    out = pl.pallas_call(
        lambda *refs: state_kernel(*refs, head_width=head_width, first=group * wide),
        grid_spec=pltpu.PrefetchScalarGridSpec(
            num_scalar_prefetch=1,
            grid=(SQUARE,),
            in_specs=[column(rows), column(edge.shape[0]), column(taps.shape[0]), whole(end), whole(bt)],
            out_specs=[pl.BlockSpec((rows, cols), lambda j, p: (0, j))] + [pl.BlockSpec((state, cols), lambda j, p: (0, 0))] * SQUARE,
            scratch_shapes=[pltpu.VMEM((rows, cols), BF16)],
        ),
        out_shape=[jax.ShapeDtypeStruct((rows, wide), BF16)] + [slot] * SQUARE,
        compiler_params=params(),
        cost_estimate=pl.CostEstimate(flops=2 * rows * wide * 2 * state, bytes_accessed=4 * rows * wide, transcendentals=rows * wide),
        name="states",
    )(place, inner, edge, taps, end, bt)
    return out[0], out[1:]


def local_kernel(x_ref, fwd_ref, inv_ref, fac_ref, mix_ref, bt_ref, out_ref, *, head_width, first):
    rows, cols = x_ref.shape
    heads = fwd_ref.shape[1] // 2
    chunks = rows // CHUNK
    for sub in range(cols // SUB):
        at_cols = pl.ds(sub * SUB, SUB)
        table = spread(heads, head_width, first + pl.program_id(0) * cols + sub * SUB, SUB)
        factors = dot(fac_ref[...], table)
        skip = factors[chunks : chunks + 1]
        state = jnp.zeros((bt_ref.shape[0], SUB), F32)
        all_scaled = (dot(inv_ref[...], table) * x_ref[:, at_cols].astype(F32)).astype(BF16)
        forward = dot(fwd_ref[...], table)
        for c in range(chunks):
            at = pl.ds(c * CHUNK, CHUNK)
            x = x_ref[at, at_cols].astype(F32)
            scaled = all_scaled[c * CHUNK : (c + 1) * CHUNK]
            both = jnp.concatenate([scaled, state.astype(BF16)], axis=0)
            mixed = dot(mix_ref[at, :], both)
            out_ref[at, at_cols] = forward[c * CHUNK : (c + 1) * CHUNK] * mixed + skip * x
            if c + 1 < chunks:
                state = factors[c : c + 1] * (state + dot(bt_ref[:, at], scaled))


def local_parts(x, fwd, inv, fac, mix, bt, head_width, group):
    rows, wide = x.shape
    cols = wide // SQUARE
    state = bt.shape[0]
    whole = lambda a: pl.BlockSpec(a.shape, lambda j: (0,) * a.ndim)
    column = pl.BlockSpec((rows, cols), lambda j: (0, j))
    return pl.pallas_call(
        lambda *refs: local_kernel(*refs, head_width=head_width, first=group * wide),
        grid=(SQUARE,),
        in_specs=[column, whole(fwd), whole(inv), whole(fac), whole(mix), whole(bt)],
        out_specs=column,
        out_shape=jax.ShapeDtypeStruct((rows, wide), F32),
        compiler_params=params(),
        cost_estimate=pl.CostEstimate(flops=2 * rows * wide * 5 * state, bytes_accessed=6 * rows * wide, transcendentals=0),
        name="local",
    )(x, fwd, inv, fac, mix, bt)


def final_kernel(place_ref, local_ref, dev_ref, mix_ref, gain_ref, *rest, head_width, first):
    slots, out_ref, state_ref = rest[:-2], rest[-2], rest[-1]
    rows, cols = local_ref.shape
    heads = dev_ref.shape[1] // 2
    step = pl.program_id(0)
    tile = step ^ place_ref[0]
    for k in range(len(slots)):

        @pl.when(step == k)
        def _():
            state_ref[...] = slots[k][...]

    mean = jnp.where(iota((SUB, SUB), 0) // head_width == iota((SUB, SUB), 1) // head_width, 1.0 / head_width, 0.0).astype(BF16)
    for sub in range(cols // SUB):
        at_cols = pl.ds(sub * SUB, SUB)
        table = spread(heads, head_width, first + tile * cols + sub * SUB, SUB)
        carried = dot(mix_ref[:, CHUNK:], state_ref[:, at_cols])
        combined = local_ref[:, at_cols] + dot(dev_ref[...], table) * carried
        squares = dot((combined * combined).astype(BF16), mean)
        out_ref[:, at_cols] = (combined * lax.rsqrt(squares + 1e-05) * gain_ref[:, at_cols]).astype(BF16)


def finish(place, local, dev, mix, gain, slots, head_width, group, into):
    rows, wide = local.shape
    cols = wide // SQUARE
    base = group * SQUARE
    whole = lambda a: pl.BlockSpec(a.shape, lambda k, p: (0,) * a.ndim)
    in_specs = [
        pl.BlockSpec((rows, cols), lambda k, p: (0, k ^ p[0])),
        whole(dev),
        whole(mix),
        pl.BlockSpec((1, cols), lambda k, p: (0, base + (k ^ p[0]))),
    ] + [whole(s) for s in slots]
    operands = [place, local, dev, mix, gain, *slots]
    aliases = {}
    if into is not None:
        in_specs.append(pl.BlockSpec(memory_space=pl.ANY))
        operands.append(into)
        aliases = {len(operands) - 1: 0}

    def kernel(*refs):
        count = 5 + len(slots)
        skipped = 0 if into is None else 1
        final_kernel(*refs[:count], *refs[count + skipped :], head_width=head_width, first=group * wide)

    return pl.pallas_call(
        kernel,
        grid_spec=pltpu.PrefetchScalarGridSpec(
            num_scalar_prefetch=1,
            grid=(SQUARE,),
            in_specs=in_specs,
            out_specs=pl.BlockSpec((rows, cols), lambda k, p: (0, base + (k ^ p[0]))),
            scratch_shapes=[pltpu.VMEM(slots[0].shape, BF16)],
        ),
        out_shape=jax.ShapeDtypeStruct((rows, wide * GROUPS), BF16),
        input_output_aliases=aliases,
        compiler_params=params(),
        cost_estimate=pl.CostEstimate(flops=2 * rows * wide * 512, bytes_accessed=6 * rows * wide, transcendentals=rows * wide),
        name="finish",
    )(*operands)


def shifted(x, by):
    length = lax.axis_size("ctx")
    return lax.ppermute(x, "ctx", [(i, i + by) for i in range(length - by)])


def swapped(x, k):
    length = lax.axis_size("ctx")
    return lax.ppermute(x, "ctx", [(i, i ^ k) for i in range(length)])


def weights_kernel(place_ref, *refs, head_width):
    total_refs, out_ref = refs[:-1], refs[-1]
    groups, _, cols = out_ref.shape
    wide = total_refs[0].shape[1]
    spot = place_ref[0]
    places = [spot ^ k for k in range(SQUARE)]
    for group in range(groups):
        low = iota((wide, cols), 0) * head_width
        col = (group * SQUARE + spot) * cols + iota((wide, cols), 1)
        table = jnp.where((col >= low) & (col < low + head_width), 1.0, 0.0)
        logs = [exact_dot(ref[...], table)[:1] for ref in total_refs]
        between = lambda low, high: sum(jnp.where((at > low) & (at < high), log, 0.0) for at, log in zip(places, logs))
        for k, end in enumerate(places + [SQUARE]):
            for q in range(SQUARE):
                weight = jnp.where(places[q] < end, jnp.exp(between(places[q], end)), 0.0)
                out_ref[group, k * SQUARE + q : k * SQUARE + q + 1, :] = weight
        for k in range(SQUARE):
            row = SQUARE * (SQUARE + 1) + k
            out_ref[group, row : row + 1, :] = jnp.exp(between(-1, places[k]))
        row = SQUARE * (SQUARE + 2)
        out_ref[group, row : row + 1, :] = sum(logs)


def square_weights(place, totals, width, head_width):
    cols = width // (GROUPS * SQUARE)
    return pl.pallas_call(
        lambda *refs: weights_kernel(*refs, head_width=head_width),
        grid_spec=pltpu.PrefetchScalarGridSpec(
            num_scalar_prefetch=1,
            grid=(1,),
            in_specs=[pl.BlockSpec(t.shape, lambda i, p: (0, 0)) for t in totals],
            out_specs=pl.BlockSpec((GROUPS, 32, cols), lambda i, p: (0, 0, 0)),
        ),
        out_shape=jax.ShapeDtypeStruct((GROUPS, 32, cols), F32),
        compiler_params=params(),
        name="weights",
    )(place, *totals)


def previous_squares(leaving, total):
    squares = lax.axis_size("ctx") // SQUARE
    entering = shifted(leaving, SQUARE)
    span = 1
    if squares > 2:
        window = shifted(total, SQUARE)
    while span < squares - 1:
        behind = shifted(entering, SQUARE * span)
        entering = (entering.astype(F32) + jnp.exp(window) * behind.astype(F32)).astype(BF16)
        window = window + shifted(window, SQUARE * span)
        span *= 2
    return entering


def body(inner_input, state_proj, step_size, decay_log, conv_inner, conv_proj, skip_weight, norm_gain):
    rows, width = inner_input.shape
    heads = step_size.shape[1]
    head_width = width // heads
    place = jnp.full((1,), lax.axis_index("ctx") % SQUARE, jnp.int32)
    edge = shifted(jnp.concatenate([inner_input[rows - EDGE :], state_proj[rows - EDGE :]], axis=1), 1)
    fwd, inv, dev, end, fac, total = decays(decay_log, step_size, skip_weight)
    totals = [total] + [swapped(total, k) for k in range(1, SQUARE)]
    mix, bt = projections(state_proj, edge, conv_proj)
    gain = norm_gain[None]
    xs, sent = [], []
    for group in range(GROUPS):
        x, slots = device_states(place, inner_input, edge, conv_inner, end, bt, head_width, group)
        xs.append(x)
        sent.append([slots[0]] + [swapped(slots[k], k) for k in range(1, SQUARE)])
    weights = square_weights(place, totals, width, head_width)
    returned, locals_ = [], []
    for group in range(GROUPS):
        x = xs[group]
        if group:
            x, leaving = lax.optimization_barrier((x, leaving))
        locals_.append(local_parts(x, fwd, inv, fac, mix, bt, head_width, group))
        w = [weights[group, r : r + 1] for r in range(SQUARE * (SQUARE + 2) + 1)]
        held = [s.astype(F32) for s in sent[group]]
        prefix = [sum(w[k * SQUARE + q] * held[q] for q in range(SQUARE)) for k in range(SQUARE + 1)]
        leaving = prefix[SQUARE].astype(BF16)
        arrived = previous_squares(leaving, w[SQUARE * (SQUARE + 2)]).astype(F32)
        entering = [(prefix[k] + w[SQUARE * (SQUARE + 1) + k] * arrived).astype(BF16) for k in range(SQUARE)]
        returned.append([entering[0]] + [swapped(entering[k], k) for k in range(1, SQUARE)])
    out = None
    for group in range(GROUPS):
        out = finish(place, locals_[group], dev, mix, gain, returned[group], head_width, group, out)
    return out


def solution(mesh):
    split = P(("dp", "ctx"), None)
    return jax.shard_map(
        body, mesh=mesh, in_specs=(split, split, split, split, P(), P(), P(), P()), out_specs=split, check_vma=False
    )
```

```python
import jax
import jax.numpy as jnp
from jax import lax
from jax.experimental import pallas as pl
from jax.experimental.pallas import tpu as pltpu
from jax.sharding import PartitionSpec as P

CHUNK = 128
SQUARE = 4
GROUPS = 2
SUB = 256
EDGE = 16
LANES = 128
F32 = jnp.float32
BF16 = jnp.bfloat16


def params(mib=16):
    return pltpu.CompilerParams(vmem_limit_bytes=mib * 1024 * 1024)


def dot(a, b):
    return jnp.dot(a, b, preferred_element_type=F32)


def dot_rows(a, b):
    return lax.dot_general(a, b, (((1,), (1,)), ((), ())), preferred_element_type=F32)


def pieces(value, count):
    out = []
    for _ in range(count):
        out.append(value.astype(BF16))
        value = value - out[-1].astype(F32)
    return out


def iota(shape, axis):
    return lax.broadcasted_iota(jnp.int32, shape, axis)


def hint(moved):
    return pl.CostEstimate(flops=0, bytes_accessed=moved, transcendentals=0)


def vmem():
    return pl.BlockSpec(memory_space=pltpu.VMEM)


def smem():
    return pl.BlockSpec(memory_space=pltpu.SMEM)


def anywhere():
    return pl.BlockSpec(memory_space=pl.ANY)


def over_heads(values, head_width, first, cols):
    blocks = []
    for lane in range(0, cols, LANES):
        head = (first + lane + iota(values.shape, 1)) // head_width
        blocks.append(jnp.take_along_axis(values, head, axis=1, mode="promise_in_bounds"))
    return jnp.concatenate(blocks, axis=1)


def silu_conv(rows_back, taps):
    count = len(taps)
    half = sum(rows_back(k) * (0.5 * taps[count - 1 - k]) for k in range(count))
    return half + half * jnp.tanh(half)


def edges_kernel(inner_ref, proj_ref, out_ref, sems):
    width = inner_ref.shape[1]
    last = pl.ds(inner_ref.shape[0] - EDGE, EDGE)
    copies = [
        pltpu.make_async_copy(inner_ref.at[last, :], out_ref.at[:, :width], sems.at[0]),
        pltpu.make_async_copy(proj_ref.at[last, :], out_ref.at[:, width:], sems.at[1]),
    ]
    for copy in copies:
        copy.start()
    for copy in copies:
        copy.wait()


def last_rows(inner, proj):
    width = inner.shape[1] + proj.shape[1]
    return pl.pallas_call(
        edges_kernel,
        in_specs=[anywhere()] * 2,
        out_specs=vmem(),
        out_shape=jax.ShapeDtypeStruct((EDGE, width), BF16),
        scratch_shapes=[pltpu.SemaphoreType.DMA((2,))],
        compiler_params=params(),
        name="edges",
    )(inner, proj)


def decay_kernel(decay_ref, step_ref, skip_ref, fwd_ref, inv_ref, dev_ref, end_ref, fac_ref):
    heads, rows = decay_ref.shape
    chunks = rows // CHUNK
    lower = jnp.where(iota((CHUNK, CHUNK), 0) >= iota((CHUNK, CHUNK), 1), 1.0, 0.0).astype(BF16)
    same = jnp.where(iota((CHUNK, CHUNK), 0) == iota((CHUNK, CHUNK), 1), 1.0, 0.0).astype(BF16)
    copies = LANES // heads
    cums, steps = [], []
    for c in range(chunks):
        at = pl.ds(c * CHUNK, CHUNK)
        decay = jnp.concatenate([decay_ref[:, at]] * copies, axis=0)
        step = jnp.concatenate([step_ref[:, at]] * copies, axis=0)
        cums.append(sum(dot_rows(lower, piece) for piece in pieces(decay, 3)))
        steps.append(sum(dot_rows(same, piece) for piece in pieces(step, 3)))
    totals = [cum[CHUNK - 1 :] for cum in cums]
    middles = [cum[CHUNK // 2 - 1 : CHUNK // 2] for cum in cums]
    before = [jnp.zeros_like(totals[0])]
    for c in range(chunks):
        before.append(before[c] + totals[c])
    after = [jnp.zeros_like(totals[0])]
    for c in range(chunks - 1, 0, -1):
        after.insert(0, after[0] + totals[c])
    fac_ref[...] = jnp.zeros_like(fac_ref)
    for c in range(chunks):
        at = pl.ds(c * CHUNK, CHUNK)
        fwd_ref[at, :] = jnp.exp(cums[c] - middles[c])
        inv_ref[at, :] = jnp.exp(middles[c] - cums[c]) * steps[c]
        dev_ref[at, :] = jnp.exp(before[c] + cums[c])
        end_ref[at, :] = jnp.exp((totals[c] - cums[c]) + after[c]) * steps[c]
        following = middles[c + 1] if c + 1 < chunks else 0.0
        fac_ref[c : c + 1, :] = jnp.exp(totals[c] - middles[c] + following)
    fac_ref[chunks : chunks + 1, :] = skip_ref[:1]
    fac_ref[8:9, :] = jnp.exp(before[chunks])


def decays(decay_log, step_size, skip_weight):
    rows, heads = decay_log.shape
    wide = jax.ShapeDtypeStruct((rows, LANES), F32)
    return pl.pallas_call(
        decay_kernel,
        out_shape=(wide, wide, wide, wide, jax.ShapeDtypeStruct((16, LANES), F32)),
        compiler_params=params(),
        name="decays",
    )(decay_log.T, step_size.T, jnp.broadcast_to(jnp.tile(skip_weight, LANES // heads)[None], (8, LANES)))


def project(proj_ref, edge_ref, taps_ref, mix_ref, bt_ref, wide_ref):
    rows, width = proj_ref.shape
    state = width // 2
    taps = [taps_ref[k : k + 1, :] for k in range(taps_ref.shape[0])]
    causal = iota((CHUNK, CHUNK), 0) >= iota((CHUNK, CHUNK), 1)
    past = edge_ref.shape[0]
    wide_ref[EDGE - past : EDGE, :] = edge_ref[:, edge_ref.shape[1] - width :].astype(F32)
    wide_ref[EDGE:, :] = proj_ref[...].astype(F32)
    for c in range(rows // CHUNK):
        at = pl.ds(c * CHUNK, CHUNK)
        both = silu_conv(lambda k: wide_ref[pl.ds(EDGE + c * CHUNK - k, CHUNK), :], taps).astype(BF16)
        b_rows, c_rows = both[:, :state], both[:, state:]
        mix_ref[at, :CHUNK] = jnp.where(causal, dot_rows(c_rows, b_rows), 0.0).astype(BF16)
        mix_ref[at, CHUNK:] = c_rows
        bt_ref[:, at] = b_rows.astype(F32).T.astype(BF16)


def summarize(place_ref, in_ref, ready, edge_ref, taps_ref, end_ref, fac_ref, bt_ref, x_ref, slots, window_ref, sum_ref, head_width, first):
    rows, wide = x_ref.shape
    cols = wide // SQUARE
    state = bt_ref.shape[0]
    count = taps_ref.shape[0]
    chunks = rows // CHUNK
    blocks = wide // LANES
    for block in range(blocks):
        at_lanes = pl.ds(first + block * LANES, LANES)
        window_ref[block, EDGE + CHUNK - count + 1 :, :] = edge_ref[:, at_lanes].astype(F32)
    sum_ref[...] = jnp.zeros_like(sum_ref)

    def chunk_step(c, _):
        ready(c)
        at = pl.ds(pl.multiple_of(c * CHUNK, CHUNK), CHUNK)
        for sub in range(wide // SUB):
            at_cols = pl.ds(sub * SUB, SUB)
            here = first + sub * SUB
            rows_here = in_ref[at, at_cols].astype(F32)
            xs = []
            for lane in range(0, SUB, LANES):
                block = (sub * SUB + lane) // LANES
                window_ref[block, EDGE - 8 : EDGE, :] = window_ref[block, EDGE + CHUNK - 8 :, :]
                window_ref[block, EDGE:, :] = rows_here[:, lane : lane + LANES]
                taps = [taps_ref[k : k + 1, pl.ds(here + lane, LANES)] for k in range(count)]
                xs.append(silu_conv(lambda k: window_ref[block, pl.ds(EDGE - k, CHUNK), :], taps))
            x = jnp.concatenate(xs, axis=1)
            x_ref[at, at_cols] = x.astype(BF16)
            scaled = (over_heads(end_ref[at, :], head_width, here, SUB) * x).astype(BF16)
            sum_ref[:, at_cols] += dot(bt_ref[:, at], scaled)
        return 0

    lax.fori_loop(0, chunks, chunk_step, 0)
    row = iota((EDGE, cols), 0)
    decay_rows = fac_ref[8:16, :]
    for k, slot in enumerate(slots):
        start = pl.multiple_of((k ^ place_ref[0]) * cols, cols)
        slot[:state, :] = sum_ref[:, pl.ds(start, cols)].astype(BF16)
        decay = over_heads(decay_rows, head_width, first + start, cols)[:1]
        high = decay.astype(BF16).astype(F32)
        slot[state:, :] = jnp.where(row == 0, high, jnp.where(row == 1, decay - high, 0.0)).astype(BF16)


def first_kernel(place_ref, in_ref, proj_ref, edge_ref, taps_ref, proj_taps_ref, end_ref, fac_ref, x_ref, later_ref, mix_ref, bt_ref, *rest, head_width):
    slots, (block_ref, wide_ref, window_ref, sum_ref, sems, later_sem) = rest[:SQUARE], rest[SQUARE:]
    rows, wide = x_ref.shape

    def fetch(c):
        at = pl.ds(pl.multiple_of(c * CHUNK, CHUNK), CHUNK)
        return pltpu.make_async_copy(in_ref.at[at, pl.ds(0, wide)], block_ref.at[at, :], sems.at[c])

    for c in range(rows // CHUNK):
        fetch(c).start()
    later = pltpu.make_async_copy(in_ref.at[:, pl.ds(wide, later_ref.shape[1])], later_ref, later_sem)
    later.start()
    project(proj_ref, edge_ref, proj_taps_ref, mix_ref, bt_ref, wide_ref)
    summarize(place_ref, block_ref, lambda c: fetch(c).wait(), edge_ref, taps_ref, end_ref, fac_ref, bt_ref, x_ref, slots, window_ref, sum_ref, head_width, 0)
    later.wait()


def slot_shapes(state, wide):
    return [jax.ShapeDtypeStruct((state + EDGE, wide // SQUARE), BF16)] * SQUARE


def sum_scratch(state, wide):
    return [pltpu.VMEM((wide // LANES, EDGE + CHUNK, LANES), F32), pltpu.VMEM((state, wide), F32)]


def first_states(place, inner, proj, edge, taps, proj_taps, end, fac, head_width):
    rows, width = inner.shape
    state = proj.shape[1] // 2
    wide = width // GROUPS
    chunks = rows // CHUNK
    out = pl.pallas_call(
        lambda *refs: first_kernel(*refs, head_width=head_width),
        in_specs=[smem(), pl.BlockSpec(memory_space=pltpu.HBM)] + [vmem()] * 6,
        out_specs=[vmem()] * (SQUARE + 4),
        out_shape=[
            jax.ShapeDtypeStruct((rows, wide), BF16),
            jax.ShapeDtypeStruct((rows, width - wide), BF16),
            jax.ShapeDtypeStruct((rows, CHUNK + state), BF16),
            jax.ShapeDtypeStruct((state, rows), BF16),
        ]
        + slot_shapes(state, wide),
        scratch_shapes=[pltpu.VMEM((rows, wide), BF16), pltpu.VMEM((EDGE + rows, 2 * state), F32)]
        + sum_scratch(state, wide)
        + [pltpu.SemaphoreType.DMA((chunks,)), pltpu.SemaphoreType.DMA],
        compiler_params=params(),
        cost_estimate=hint(4 * rows * wide),
        name="first_states",
    )(place, inner, proj, edge, taps, proj_taps, end, fac)
    return out[:4], out[4:]


def later_kernel(place_ref, in_ref, edge_ref, taps_ref, end_ref, fac_ref, bt_ref, x_ref, *rest, head_width, first):
    slots, (window_ref, sum_ref) = rest[:SQUARE], rest[SQUARE:]
    summarize(place_ref, in_ref, lambda c: None, edge_ref, taps_ref, end_ref, fac_ref, bt_ref, x_ref, slots, window_ref, sum_ref, head_width, first)


def later_states(place, inner, edge, taps, end, fac, bt, head_width):
    rows, wide = inner.shape
    state = bt.shape[0]
    first = taps.shape[1] - wide
    out = pl.pallas_call(
        lambda *refs: later_kernel(*refs, head_width=head_width, first=first),
        in_specs=[smem()] + [vmem()] * 6,
        out_specs=[vmem()] * (SQUARE + 1),
        out_shape=[jax.ShapeDtypeStruct((rows, wide), BF16)] + slot_shapes(state, wide),
        scratch_shapes=sum_scratch(state, wide),
        compiler_params=params(),
        cost_estimate=hint(4 * rows * wide),
        name="later_states",
    )(place, inner, edge, taps, end, fac, bt)
    return out[0], out[1:]


def combine_kernel(place_ref, *refs):
    slots, (leaving_ref, prefix_ref, opening_ref, placed_ref) = refs[:SQUARE], refs[SQUARE:]
    state, cols = leaving_ref.shape
    spot = place_ref[0]
    for k in range(SQUARE):
        placed_ref[spot ^ k] = slots[k][...]
    running = jnp.zeros((state, cols), F32)
    opening = jnp.ones((1, cols), F32)
    for p in range(SQUARE):
        prefix_ref[spot ^ p] = running
        opening_ref[spot ^ p] = jnp.broadcast_to(opening, (8, cols))
        tail = placed_ref[p, state:, :].astype(F32)
        decay = tail[0:1] + tail[1:2]
        running = decay * running + placed_ref[p, :state, :].astype(F32)
        opening = decay * opening
    leaving_ref[...] = running.astype(BF16)
    opening_ref[SQUARE] = jnp.broadcast_to(opening, (8, cols))


def combine(place, slots):
    rows, cols = slots[0].shape
    state = rows - EDGE
    return pl.pallas_call(
        combine_kernel,
        in_specs=[smem()] + [vmem()] * SQUARE,
        out_specs=[vmem()] * 3,
        out_shape=(
            jax.ShapeDtypeStruct((state, cols), BF16),
            jax.ShapeDtypeStruct((SQUARE, state, cols), F32),
            jax.ShapeDtypeStruct((SQUARE + 1, 8, cols), F32),
        ),
        scratch_shapes=[pltpu.VMEM((SQUARE, rows, cols), BF16)],
        compiler_params=params(),
        name="combine",
    )(place, *slots)


def local_kernel(x_ref, fwd_ref, inv_ref, fac_ref, mix_ref, bt_ref, out_ref, *, head_width, first):
    rows, wide = x_ref.shape
    chunks = rows // CHUNK
    cols = wide // SQUARE

    def tile_step(j, _):
        base = pl.multiple_of(j * cols, cols)
        for sub in range(cols // SUB):
            at_cols = pl.ds(base + sub * SUB, SUB)
            here = first + base + sub * SUB
            factors = over_heads(fac_ref[...], head_width, here, SUB)
            skip = factors[chunks : chunks + 1]
            state = jnp.zeros((bt_ref.shape[0], SUB), F32)
            for c in range(chunks):
                at = pl.ds(c * CHUNK, CHUNK)
                x = x_ref[at, at_cols].astype(F32)
                scaled = (over_heads(inv_ref[at, :], head_width, here, SUB) * x).astype(BF16)
                both = jnp.concatenate([scaled, state.astype(BF16)], axis=0)
                mixed = dot(mix_ref[at, :], both)
                out_ref[at, at_cols] = over_heads(fwd_ref[at, :], head_width, here, SUB) * mixed + skip * x
                if c + 1 < chunks:
                    state = factors[c : c + 1] * (state + dot(bt_ref[:, at], scaled))
        return 0

    lax.fori_loop(0, SQUARE, tile_step, 0)


def local_parts(x, fwd, inv, fac, mix, bt, head_width, group):
    rows, wide = x.shape
    state = bt.shape[0]
    return pl.pallas_call(
        lambda *refs: local_kernel(*refs, head_width=head_width, first=group * wide),
        in_specs=[vmem()] * 6,
        out_specs=vmem(),
        out_shape=jax.ShapeDtypeStruct((rows, wide), F32),
        compiler_params=params(),
        cost_estimate=pl.CostEstimate(flops=2 * rows * wide * 5 * state, bytes_accessed=6 * rows * wide, transcendentals=0),
        name="local",
    )(x, fwd, inv, fac, mix, bt)


def final_kernel(place_ref, local_ref, dev_ref, mix_ref, gain_ref, *rest, head_width, first):
    slots, (out_ref, stage_ref, sems) = rest[:SQUARE], rest[-3:]
    rows, wide = local_ref.shape
    cols = wide // SQUARE
    mean = jnp.where(iota((SUB, SUB), 0) // head_width == iota((SUB, SUB), 1) // head_width, 1.0 / head_width, 0.0).astype(BF16)
    copies = []
    for k in range(SQUARE):
        base = pl.multiple_of((k ^ place_ref[0]) * cols, cols)
        for sub in range(cols // SUB):
            at_cols = pl.ds(base + sub * SUB, SUB)
            carried = dot(mix_ref[:, CHUNK:], slots[k][:, sub * SUB : (sub + 1) * SUB])
            combined = local_ref[:, at_cols] + over_heads(dev_ref[...], head_width, first + base + sub * SUB, SUB) * carried
            squares = dot((combined * combined).astype(BF16), mean)
            gain = gain_ref[:, pl.ds(first + base + sub * SUB, SUB)]
            turn = k * (cols // SUB) + sub
            stage_ref[turn] = (combined * lax.rsqrt(squares + 1e-05) * gain).astype(BF16)
            copies.append(pltpu.make_async_copy(stage_ref.at[turn], out_ref.at[:, pl.ds(first + base + sub * SUB, SUB)], sems.at[turn]))
            copies[-1].start()
    for copy in copies:
        copy.wait()


def finish(place, local, dev, mix, gain, slots, head_width, group, into):
    rows, wide = local.shape
    operands = [place, local, dev, mix, gain, *slots]
    in_specs = [smem()] + [vmem()] * (len(operands) - 1)
    aliases = {}
    if into is not None:
        in_specs.append(anywhere())
        operands.append(into)
        aliases = {len(operands) - 1: 0}
    return pl.pallas_call(
        lambda *refs: final_kernel(*refs, head_width=head_width, first=group * wide),
        in_specs=in_specs,
        out_specs=anywhere(),
        out_shape=jax.ShapeDtypeStruct((rows, wide * GROUPS), BF16),
        scratch_shapes=[pltpu.VMEM((wide // SUB, rows, SUB), BF16), pltpu.SemaphoreType.DMA((wide // SUB,))],
        input_output_aliases=aliases,
        compiler_params=params(),
        cost_estimate=pl.CostEstimate(flops=2 * rows * wide * 512, bytes_accessed=6 * rows * wide, transcendentals=rows * wide),
        name="finish",
    )(*operands)


def shifted(x, by):
    length = lax.axis_size("ctx")
    return lax.ppermute(x, "ctx", [(i, i + by) for i in range(length - by)])


def swapped(x, k):
    length = lax.axis_size("ctx")
    return lax.ppermute(x, "ctx", [(i, i ^ k) for i in range(length)])


def previous_squares(leaving, decay):
    squares = lax.axis_size("ctx") // SQUARE
    entering = shifted(leaving, SQUARE)
    span = 1
    if squares > 2:
        window = shifted(decay, SQUARE)
    while span < squares - 1:
        behind = shifted(entering, SQUARE * span)
        entering = (entering.astype(F32) + window * behind.astype(F32)).astype(BF16)
        window = window * shifted(window, SQUARE * span)
        span *= 2
    return entering


def body(inner_input, state_proj, step_size, decay_log, conv_inner, conv_proj, skip_weight, norm_gain):
    rows, width = inner_input.shape
    heads = step_size.shape[1]
    head_width = width // heads
    past = conv_inner.shape[0] - 1
    kept = pltpu.with_memory_space_constraint(inner_input, pltpu.HBM)
    place = jnp.full((1,), lax.axis_index("ctx") % SQUARE, jnp.int32)
    edge = shifted(last_rows(kept, state_proj)[EDGE - past :], 1)
    fwd, inv, dev, end, fac = decays(decay_log, step_size, skip_weight)
    gain = norm_gain[None]
    (x, later, mix, bt), slots = first_states(place, kept, state_proj, edge, conv_inner, conv_proj, end, fac, head_width)
    xs, sent = [x], [[slots[0]] + [swapped(slots[k], k) for k in range(1, SQUARE)]]
    x, slots = later_states(place, later, edge, conv_inner, end, fac, bt, head_width)
    xs.append(x)
    sent.append([slots[0]] + [swapped(slots[k], k) for k in range(1, SQUARE)])
    returned, locals_ = [], []
    for group in range(GROUPS):
        x = xs[group]
        if group:
            x, leaving = lax.optimization_barrier((x, leaving))
        locals_.append(local_parts(x, fwd, inv, fac, mix, bt, head_width, group))
        leaving, prefix, opening = combine(place, sent[group])
        arrived = previous_squares(leaving, opening[SQUARE, :1]).astype(F32)
        entering = [(prefix[k] + opening[k, :1] * arrived).astype(BF16) for k in range(SQUARE)]
        returned.append([entering[0]] + [swapped(entering[k], k) for k in range(1, SQUARE)])
    out = None
    for group in range(GROUPS):
        out = finish(place, locals_[group], dev, mix, gain, returned[group], head_width, group, out)
    return out


def solution(mesh):
    split = P(("dp", "ctx"), None)
    return jax.shard_map(
        body, mesh=mesh, in_specs=(split, split, split, split, P(), P(), P(), P()), out_specs=split, check_vma=False
    )
```

```python
import jax
import jax.numpy as jnp
from jax import lax
from jax.experimental import pallas as pl
from jax.experimental.pallas import tpu as pltpu
from jax.sharding import PartitionSpec as P

CHUNK = 128
SQUARE = 4
GROUPS = 2
SUB = 256
EDGE = 16
LANES = 128
F32 = jnp.float32
BF16 = jnp.bfloat16


def params(mib=16):
    return pltpu.CompilerParams(vmem_limit_bytes=mib * 1024 * 1024)


def dot(a, b):
    return jnp.dot(a, b, preferred_element_type=F32)


def dot_rows(a, b):
    return lax.dot_general(a, b, (((1,), (1,)), ((), ())), preferred_element_type=F32)


def pieces(value, count):
    out = []
    for _ in range(count):
        out.append(value.astype(BF16))
        value = value - out[-1].astype(F32)
    return out


def iota(shape, axis):
    return lax.broadcasted_iota(jnp.int32, shape, axis)


def hint(moved):
    return pl.CostEstimate(flops=0, bytes_accessed=moved, transcendentals=0)


def vmem():
    return pl.BlockSpec(memory_space=pltpu.VMEM)


def smem():
    return pl.BlockSpec(memory_space=pltpu.SMEM)


def anywhere():
    return pl.BlockSpec(memory_space=pl.ANY)


def over_heads(values, head_width, first, cols):
    blocks = []
    for lane in range(0, cols, LANES):
        head = (first + lane + iota(values.shape, 1)) // head_width
        blocks.append(jnp.take_along_axis(values, head, axis=1, mode="promise_in_bounds"))
    return jnp.concatenate(blocks, axis=1)


def silu_conv(rows_back, taps):
    count = len(taps)
    half = sum(rows_back(k) * (0.5 * taps[count - 1 - k]) for k in range(count))
    return half + half * jnp.tanh(half)


def edges_kernel(inner_ref, proj_ref, out_ref, sems):
    width = inner_ref.shape[1]
    last = pl.ds(inner_ref.shape[0] - EDGE, EDGE)
    copies = [
        pltpu.make_async_copy(inner_ref.at[last, :], out_ref.at[:, :width], sems.at[0]),
        pltpu.make_async_copy(proj_ref.at[last, :], out_ref.at[:, width:], sems.at[1]),
    ]
    for copy in copies:
        copy.start()
    for copy in copies:
        copy.wait()


def last_rows(inner, proj):
    width = inner.shape[1] + proj.shape[1]
    return pl.pallas_call(
        edges_kernel,
        in_specs=[anywhere()] * 2,
        out_specs=vmem(),
        out_shape=jax.ShapeDtypeStruct((EDGE, width), BF16),
        scratch_shapes=[pltpu.SemaphoreType.DMA((2,))],
        compiler_params=params(),
        name="edges",
    )(inner, proj)


def first_chunk(in_ref, head_ref, sem, first):
    return pltpu.make_async_copy(in_ref.at[pl.ds(0, CHUNK), pl.ds(first, head_ref.shape[1])], head_ref, sem)


def decay_kernel(decay_ref, step_ref, skip_ref, inner_ref, fwd_ref, inv_ref, dev_ref, fac_ref, head_ref, sem):
    head = first_chunk(inner_ref, head_ref, sem, 0)
    head.start()
    heads, rows = decay_ref.shape
    chunks = rows // CHUNK
    lower = jnp.where(iota((CHUNK, CHUNK), 0) >= iota((CHUNK, CHUNK), 1), 1.0, 0.0).astype(BF16)
    same = jnp.where(iota((CHUNK, CHUNK), 0) == iota((CHUNK, CHUNK), 1), 1.0, 0.0).astype(BF16)
    copies = LANES // heads
    cums, steps = [], []
    for c in range(chunks):
        at = pl.ds(c * CHUNK, CHUNK)
        decay = jnp.concatenate([decay_ref[:, at]] * copies, axis=0)
        step = jnp.concatenate([step_ref[:, at]] * copies, axis=0)
        cums.append(sum(dot_rows(lower, piece) for piece in pieces(decay, 3)))
        steps.append(sum(dot_rows(same, piece) for piece in pieces(step, 3)))
    totals = [cum[CHUNK - 1 :] for cum in cums]
    middles = [cum[CHUNK // 2 - 1 : CHUNK // 2] for cum in cums]
    before = [jnp.zeros_like(totals[0])]
    for c in range(chunks):
        before.append(before[c] + totals[c])
    fac_ref[...] = jnp.zeros_like(fac_ref)
    for c in range(chunks):
        at = pl.ds(c * CHUNK, CHUNK)
        fwd_ref[at, :] = jnp.exp(cums[c] - middles[c])
        inv_ref[at, :] = jnp.exp(middles[c] - cums[c]) * steps[c]
        dev_ref[at, :] = jnp.exp(before[c] + cums[c])
        following = middles[c + 1] if c + 1 < chunks else 0.0
        fac_ref[c : c + 1, :] = jnp.exp(totals[c] - middles[c] + following)
    fac_ref[chunks : chunks + 1, :] = skip_ref[:1]
    fac_ref[8:9, :] = jnp.exp(before[chunks])
    head.wait()


def decays(decay_log, step_size, skip_weight, inner):
    rows, heads = decay_log.shape
    wide = jax.ShapeDtypeStruct((rows, LANES), F32)
    return pl.pallas_call(
        decay_kernel,
        in_specs=[vmem()] * 3 + [anywhere()],
        out_specs=[vmem()] * 5,
        out_shape=(wide, wide, wide, jax.ShapeDtypeStruct((16, LANES), F32), jax.ShapeDtypeStruct((CHUNK, inner.shape[1] // GROUPS), BF16)),
        scratch_shapes=[pltpu.SemaphoreType.DMA],
        compiler_params=params(),
        name="decays",
    )(decay_log.T, step_size.T, jnp.broadcast_to(jnp.tile(skip_weight, LANES // heads)[None], (8, LANES)), inner)


def project(proj_ref, edge_ref, taps_ref, mix_ref, bt_ref, wide_ref):
    rows, width = proj_ref.shape
    state = width // 2
    taps = [taps_ref[k : k + 1, :] for k in range(taps_ref.shape[0])]
    causal = iota((CHUNK, CHUNK), 0) >= iota((CHUNK, CHUNK), 1)
    past = edge_ref.shape[0]
    wide_ref[EDGE - past : EDGE, :] = edge_ref[:, edge_ref.shape[1] - width :].astype(F32)
    wide_ref[EDGE:, :] = proj_ref[...].astype(F32)
    for c in range(rows // CHUNK):
        at = pl.ds(c * CHUNK, CHUNK)
        both = silu_conv(lambda k: wide_ref[pl.ds(EDGE + c * CHUNK - k, CHUNK), :], taps).astype(BF16)
        b_rows, c_rows = both[:, :state], both[:, state:]
        mix_ref[at, :CHUNK] = jnp.where(causal, dot_rows(c_rows, b_rows), 0.0).astype(BF16)
        mix_ref[at, CHUNK:] = c_rows
        bt_ref[:, at] = b_rows.astype(F32).T.astype(BF16)


def summarize(place_ref, in_ref, ready, edge_ref, taps_ref, inv_ref, fac_ref, bt_ref, x_ref, scaled_ref, opening_ref, slots, window_ref, sum_ref, row_ref, head_width, first):
    rows, wide = x_ref.shape
    cols = wide // SQUARE
    state = bt_ref.shape[0]
    count = taps_ref.shape[0]
    chunks = rows // CHUNK
    for block in range(wide // LANES):
        at_lanes = pl.ds(first + block * LANES, LANES)
        window_ref[block, EDGE + CHUNK - count + 1 :, :] = edge_ref[:, at_lanes].astype(F32)
    row_ref[...] = over_heads(fac_ref[...], head_width, first, wide)
    sum_ref[...] = jnp.zeros_like(sum_ref)

    def chunk_step(c, _):
        ready(c)
        at = pl.ds(pl.multiple_of(c * CHUNK, CHUNK), CHUNK)
        for sub in range(wide // SUB):
            at_cols = pl.ds(sub * SUB, SUB)
            here = first + sub * SUB
            rows_here = in_ref[at, at_cols].astype(F32)
            xs = []
            for lane in range(0, SUB, LANES):
                block = (sub * SUB + lane) // LANES
                window_ref[block, EDGE - 8 : EDGE, :] = window_ref[block, EDGE + CHUNK - 8 :, :]
                window_ref[block, EDGE:, :] = rows_here[:, lane : lane + LANES]
                taps = [taps_ref[k : k + 1, pl.ds(here + lane, LANES)] for k in range(count)]
                xs.append(silu_conv(lambda k: window_ref[block, pl.ds(EDGE - k, CHUNK), :], taps))
            x = jnp.concatenate(xs, axis=1)
            x_ref[at, at_cols] = x.astype(BF16)
            scaled = (over_heads(inv_ref[at, :], head_width, here, SUB) * x).astype(BF16)
            scaled_ref[at, at_cols] = scaled
            running = sum_ref[:, at_cols]
            opening_ref[at, at_cols] = running.astype(BF16)
            sum_ref[:, at_cols] = row_ref[pl.ds(c, 1), at_cols] * (running + dot(bt_ref[:, at], scaled))
        return 0

    lax.fori_loop(0, chunks, chunk_step, 0)
    row = iota((EDGE, cols), 0)
    for k, slot in enumerate(slots):
        start = pl.multiple_of((k ^ place_ref[0]) * cols, cols)
        slot[:state, :] = sum_ref[:, pl.ds(start, cols)].astype(BF16)
        decay = row_ref[8:16, pl.ds(start, cols)][:1]
        high = decay.astype(BF16).astype(F32)
        slot[state:, :] = jnp.where(row == 0, high, jnp.where(row == 1, decay - high, 0.0)).astype(BF16)


def first_kernel(place_ref, in_ref, head_ref, proj_ref, edge_ref, taps_ref, proj_taps_ref, inv_ref, fac_ref, x_ref, scaled_ref, opening_ref, mix_ref, bt_ref, next_ref, *rest, head_width):
    slots, (block_ref, wide_ref, window_ref, sum_ref, row_ref, sems) = rest[:SQUARE], rest[SQUARE:]
    rows, wide = x_ref.shape

    def fetch(c):
        at = pl.ds(pl.multiple_of(c * CHUNK, CHUNK), CHUNK)
        return pltpu.make_async_copy(in_ref.at[at, pl.ds(0, wide)], block_ref.at[at, :], sems.at[c])

    for c in range(1, rows // CHUNK):
        fetch(c).start()
    upcoming = first_chunk(in_ref, next_ref, sems.at[0], wide)
    upcoming.start()
    block_ref[:CHUNK, :] = head_ref[...]
    project(proj_ref, edge_ref, proj_taps_ref, mix_ref, bt_ref, wide_ref)
    summarize(place_ref, block_ref, lambda c: pl.when(c > 0)(lambda: fetch(c).wait()), edge_ref, taps_ref, inv_ref, fac_ref, bt_ref, x_ref, scaled_ref, opening_ref, slots, window_ref, sum_ref, row_ref, head_width, 0)
    upcoming.wait()


def slot_shapes(state, wide):
    return [jax.ShapeDtypeStruct((state + EDGE, wide // SQUARE), BF16)] * SQUARE


def sum_scratch(state, wide):
    return [pltpu.VMEM((wide // LANES, EDGE + CHUNK, LANES), F32), pltpu.VMEM((state, wide), F32), pltpu.VMEM((16, wide), F32)]


def first_states(place, inner, head, proj, edge, taps, proj_taps, inv, fac, head_width):
    rows, width = inner.shape
    state = proj.shape[1] // 2
    wide = width // GROUPS
    chunks = rows // CHUNK
    out = pl.pallas_call(
        lambda *refs: first_kernel(*refs, head_width=head_width),
        in_specs=[smem(), anywhere()] + [vmem()] * 7,
        out_specs=[vmem()] * (SQUARE + 6),
        out_shape=[
            jax.ShapeDtypeStruct((rows, wide), BF16),
            jax.ShapeDtypeStruct((rows, wide), BF16),
            jax.ShapeDtypeStruct((chunks * state, wide), BF16),
            jax.ShapeDtypeStruct((rows, CHUNK + state), BF16),
            jax.ShapeDtypeStruct((state, rows), BF16),
            jax.ShapeDtypeStruct((CHUNK, wide), BF16),
        ]
        + slot_shapes(state, wide),
        scratch_shapes=[pltpu.VMEM((rows, wide), BF16), pltpu.VMEM((EDGE + rows, 2 * state), F32)]
        + sum_scratch(state, wide)
        + [pltpu.SemaphoreType.DMA((chunks,))],
        compiler_params=params(),
        name="first_states",
    )(place, inner, head, proj, edge, taps, proj_taps, inv, fac)
    return out[:3], out[3:6], out[6:]


def later_kernel(place_ref, in_ref, head_ref, edge_ref, taps_ref, inv_ref, fac_ref, bt_ref, x_ref, scaled_ref, opening_ref, *rest, head_width, first):
    slots, (block_ref, window_ref, sum_ref, row_ref, sems) = rest[:SQUARE], rest[SQUARE:]
    rows, wide = x_ref.shape

    def fetch(c):
        at = pl.ds(pl.multiple_of(c * CHUNK, CHUNK), CHUNK)
        return pltpu.make_async_copy(in_ref.at[at, pl.ds(first, wide)], block_ref.at[at, :], sems.at[c])

    for c in range(1, rows // CHUNK):
        fetch(c).start()
    block_ref[:CHUNK, :] = head_ref[...]
    summarize(place_ref, block_ref, lambda c: pl.when(c > 0)(lambda: fetch(c).wait()), edge_ref, taps_ref, inv_ref, fac_ref, bt_ref, x_ref, scaled_ref, opening_ref, slots, window_ref, sum_ref, row_ref, head_width, first)


def later_states(place, inner, head, edge, taps, inv, fac, bt, head_width, group):
    rows, width = inner.shape
    wide = width // GROUPS
    state = bt.shape[0]
    chunks = rows // CHUNK
    out = pl.pallas_call(
        lambda *refs: later_kernel(*refs, head_width=head_width, first=group * wide),
        in_specs=[smem(), anywhere()] + [vmem()] * 6,
        out_specs=[vmem()] * (SQUARE + 3),
        out_shape=[
            jax.ShapeDtypeStruct((rows, wide), BF16),
            jax.ShapeDtypeStruct((rows, wide), BF16),
            jax.ShapeDtypeStruct((chunks * state, wide), BF16),
        ]
        + slot_shapes(state, wide),
        scratch_shapes=[pltpu.VMEM((rows, wide), BF16)] + sum_scratch(state, wide) + [pltpu.SemaphoreType.DMA((chunks,))],
        compiler_params=params(),
        name="later_states",
    )(place, inner, head, edge, taps, inv, fac, bt)
    return out[:3], out[3:]


def combine_kernel(place_ref, *refs):
    slots, (leaving_ref, prefix_ref, opening_ref, placed_ref) = refs[:SQUARE], refs[SQUARE:]
    state, cols = leaving_ref.shape
    spot = place_ref[0]
    for k in range(SQUARE):
        placed_ref[spot ^ k] = slots[k][...]
    running = jnp.zeros((state, cols), F32)
    opening = jnp.ones((1, cols), F32)
    for p in range(SQUARE):
        prefix_ref[spot ^ p] = running
        opening_ref[spot ^ p] = jnp.broadcast_to(opening, (8, cols))
        tail = placed_ref[p, state:, :].astype(F32)
        decay = tail[0:1] + tail[1:2]
        running = decay * running + placed_ref[p, :state, :].astype(F32)
        opening = decay * opening
    leaving_ref[...] = running.astype(BF16)
    opening_ref[SQUARE] = jnp.broadcast_to(opening, (8, cols))


def combine(place, slots):
    rows, cols = slots[0].shape
    state = rows - EDGE
    return pl.pallas_call(
        combine_kernel,
        in_specs=[smem()] + [vmem()] * SQUARE,
        out_specs=[vmem()] * 3,
        out_shape=(
            jax.ShapeDtypeStruct((state, cols), BF16),
            jax.ShapeDtypeStruct((SQUARE, state, cols), F32),
            jax.ShapeDtypeStruct((SQUARE + 1, 8, cols), F32),
        ),
        scratch_shapes=[pltpu.VMEM((SQUARE, rows, cols), BF16)],
        compiler_params=params(),
        name="combine",
    )(place, *slots)


def local_kernel(x_ref, scaled_ref, opening_ref, fwd_ref, fac_ref, mix_ref, out_ref, *, head_width, first):
    rows, wide = x_ref.shape
    chunks = rows // CHUNK
    state = opening_ref.shape[0] // chunks
    cols = wide // SQUARE

    def tile_step(j, _):
        base = pl.multiple_of(j * cols, cols)
        at_cols = pl.ds(base, cols)
        skip = over_heads(fac_ref[...], head_width, first + base, cols)[chunks : chunks + 1]
        for c in range(chunks):
            at = pl.ds(c * CHUNK, CHUNK)
            both = jnp.concatenate([scaled_ref[at, at_cols], opening_ref[pl.ds(c * state, state), at_cols]], axis=0)
            mixed = over_heads(fwd_ref[at, :], head_width, first + base, cols) * dot(mix_ref[at, :], both)
            out_ref[at, at_cols] = mixed + skip * x_ref[at, at_cols].astype(F32)
        return 0

    lax.fori_loop(0, SQUARE, tile_step, 0)


def local_parts(x, scaled, opening, fwd, fac, mix, head_width, group):
    rows, wide = x.shape
    return pl.pallas_call(
        lambda *refs: local_kernel(*refs, head_width=head_width, first=group * wide),
        in_specs=[vmem()] * 6,
        out_specs=vmem(),
        out_shape=jax.ShapeDtypeStruct((rows, wide), F32),
        compiler_params=params(),
        name="local",
    )(x, scaled, opening, fwd, fac, mix)


def normalize(place_ref, local_ref, dev_ref, mix_ref, gain_ref, slots, head_width, first, done):
    rows, wide = local_ref.shape
    cols = wide // SQUARE
    mean = jnp.where(iota((SUB, SUB), 0) // head_width == iota((SUB, SUB), 1) // head_width, 1.0 / head_width, 0.0).astype(BF16)
    for k in range(SQUARE):
        base = pl.multiple_of((k ^ place_ref[0]) * cols, cols)
        for sub in range(cols // SUB):
            at_cols = pl.ds(base + sub * SUB, SUB)
            here = first + base + sub * SUB
            carried = dot(mix_ref[:, CHUNK:], slots[k][:, sub * SUB : (sub + 1) * SUB])
            combined = local_ref[:, at_cols] + over_heads(dev_ref[...], head_width, here, SUB) * carried
            squares = dot((combined * combined).astype(BF16), mean)
            result = combined * lax.rsqrt(squares + 1e-05) * gain_ref[:, pl.ds(here, SUB)]
            done(k * (cols // SUB) + sub, base + sub * SUB, result.astype(BF16))


def finish_first_kernel(place_ref, local_ref, dev_ref, mix_ref, gain_ref, *rest, head_width):
    slots, out_ref = rest[:SQUARE], rest[SQUARE]

    def done(turn, column, result):
        out_ref[:, pl.ds(column, SUB)] = result

    normalize(place_ref, local_ref, dev_ref, mix_ref, gain_ref, slots, head_width, 0, done)


def finish_first(place, local, dev, mix, gain, slots, head_width):
    rows, wide = local.shape
    return pl.pallas_call(
        lambda *refs: finish_first_kernel(*refs, head_width=head_width),
        in_specs=[smem()] + [vmem()] * (4 + SQUARE),
        out_specs=vmem(),
        out_shape=jax.ShapeDtypeStruct((rows, wide), BF16),
        compiler_params=params(),
        name="finish_first",
    )(place, local, dev, mix, gain, *slots)


def finish_kernel(place_ref, local_ref, dev_ref, mix_ref, gain_ref, *rest, head_width):
    slots, (earlier_ref, out_ref, stage_ref, sems, earlier_sem) = rest[:SQUARE], rest[SQUARE:]
    first = earlier_ref.shape[1]
    earlier = pltpu.make_async_copy(earlier_ref, out_ref.at[:, pl.ds(0, first)], earlier_sem)
    earlier.start()
    copies = []

    def done(turn, column, result):
        stage_ref[turn] = result
        copies.append(pltpu.make_async_copy(stage_ref.at[turn], out_ref.at[:, pl.ds(first + column, SUB)], sems.at[turn]))
        copies[-1].start()

    normalize(place_ref, local_ref, dev_ref, mix_ref, gain_ref, slots, head_width, first, done)
    earlier.wait()
    for copy in copies:
        copy.wait()


def finish(place, local, dev, mix, gain, slots, earlier, head_width):
    rows, wide = local.shape
    return pl.pallas_call(
        lambda *refs: finish_kernel(*refs, head_width=head_width),
        in_specs=[smem()] + [vmem()] * (5 + SQUARE),
        out_specs=anywhere(),
        out_shape=jax.ShapeDtypeStruct((rows, wide * GROUPS), BF16),
        scratch_shapes=[pltpu.VMEM((wide // SUB, rows, SUB), BF16), pltpu.SemaphoreType.DMA((wide // SUB,)), pltpu.SemaphoreType.DMA],
        compiler_params=params(),
        name="finish",
    )(place, local, dev, mix, gain, *slots, earlier)


def shifted(x, by):
    length = lax.axis_size("ctx")
    return lax.ppermute(x, "ctx", [(i, i + by) for i in range(length - by)])


def swapped(x, k):
    length = lax.axis_size("ctx")
    return lax.ppermute(x, "ctx", [(i, i ^ k) for i in range(length)])


def previous_squares(leaving, decay):
    squares = lax.axis_size("ctx") // SQUARE
    entering = shifted(leaving, SQUARE)
    span = 1
    if squares > 2:
        window = shifted(decay, SQUARE)
    while span < squares - 1:
        behind = shifted(entering, SQUARE * span)
        entering = (entering.astype(F32) + window * behind.astype(F32)).astype(BF16)
        window = window * shifted(window, SQUARE * span)
        span *= 2
    return entering


def body(inner_input, state_proj, step_size, decay_log, conv_inner, conv_proj, skip_weight, norm_gain):
    rows, width = inner_input.shape
    heads = step_size.shape[1]
    head_width = width // heads
    past = conv_inner.shape[0] - 1
    kept, kept_proj = [pltpu.with_memory_space_constraint(a, pltpu.HBM) for a in (inner_input, state_proj)]
    place = jnp.full((1,), lax.axis_index("ctx") % SQUARE, jnp.int32)
    edge = shifted(last_rows(kept, kept_proj)[EDGE - past :], 1)
    fwd, inv, dev, fac, head = decays(decay_log, step_size, skip_weight, kept)
    gain = norm_gain[None]
    made, sent = [], []
    parts, (mix, bt, head), slots = first_states(place, kept, head, state_proj, edge, conv_inner, conv_proj, inv, fac, head_width)
    made.append(parts)
    sent.append([slots[0]] + [swapped(slots[k], k) for k in range(1, SQUARE)])
    parts, slots = later_states(place, kept, head, edge, conv_inner, inv, fac, bt, head_width, 1)
    made.append(parts)
    sent.append([slots[0]] + [swapped(slots[k], k) for k in range(1, SQUARE)])
    combined = [combine(place, sent[group]) for group in range(GROUPS)]
    arrived = [previous_squares(leaving, opening[SQUARE, :1]) for leaving, _, opening in combined]
    locals_ = [local_parts(*made[group], fwd, fac, mix, head_width, group) for group in range(GROUPS)]
    arrived[0], locals_[0] = lax.optimization_barrier((arrived[0], locals_[0]))
    returned = []
    for group in range(GROUPS):
        _, prefix, opening = combined[group]
        entering = [(prefix[k] + opening[k, :1] * arrived[group].astype(F32)).astype(BF16) for k in range(SQUARE)]
        returned.append([entering[0]] + [swapped(entering[k], k) for k in range(1, SQUARE)])
    earlier = finish_first(place, locals_[0], dev, mix, gain, returned[0], head_width)
    return finish(place, locals_[1], dev, mix, gain, returned[1], earlier, head_width)


def solution(mesh):
    split = P(("dp", "ctx"), None)
    return jax.shard_map(
        body, mesh=mesh, in_specs=(split, split, split, split, P(), P(), P(), P()), out_specs=split, check_vma=False
    )
```

```python
import jax
import jax.numpy as jnp
from jax import lax
from jax.experimental import pallas as pl
from jax.experimental.pallas import tpu as pltpu
from jax.sharding import PartitionSpec as P

CHUNK = 128
SQUARE = 4
GROUPS = 2
SUB = 256
EDGE = 16
LANES = 128
F32 = jnp.float32
BF16 = jnp.bfloat16


def params(mib=9):
    return pltpu.CompilerParams(vmem_limit_bytes=mib * 1024 * 1024)


def dot(a, b):
    return jnp.dot(a, b, preferred_element_type=F32)


def dot_rows(a, b):
    return lax.dot_general(a, b, (((1,), (1,)), ((), ())), preferred_element_type=F32)


def pieces(value, count):
    out = []
    for _ in range(count):
        out.append(value.astype(BF16))
        value = value - out[-1].astype(F32)
    return out


def iota(shape, axis):
    return lax.broadcasted_iota(jnp.int32, shape, axis)


def hint(moved):
    return pl.CostEstimate(flops=0, bytes_accessed=moved, transcendentals=0)


def vmem():
    return pl.BlockSpec(memory_space=pltpu.VMEM)


def smem():
    return pl.BlockSpec(memory_space=pltpu.SMEM)


def anywhere():
    return pl.BlockSpec(memory_space=pl.ANY)


def over_heads(values, head_width, first, cols):
    blocks = []
    for lane in range(0, cols, LANES):
        head = (first + lane + iota(values.shape, 1)) // head_width
        blocks.append(jnp.take_along_axis(values, head, axis=1, mode="promise_in_bounds"))
    return jnp.concatenate(blocks, axis=1)


def silu_conv(rows_back, taps):
    count = len(taps)
    half = sum(rows_back(k) * (0.5 * taps[count - 1 - k]) for k in range(count))
    return half + half * jnp.tanh(half)


def edges_kernel(inner_ref, proj_ref, out_ref, sems):
    width = inner_ref.shape[1]
    last = pl.ds(inner_ref.shape[0] - EDGE, EDGE)
    copies = [
        pltpu.make_async_copy(inner_ref.at[last, :], out_ref.at[:, :width], sems.at[0]),
        pltpu.make_async_copy(proj_ref.at[last, :], out_ref.at[:, width:], sems.at[1]),
    ]
    for copy in copies:
        copy.start()
    for copy in copies:
        copy.wait()


def last_rows(inner, proj):
    width = inner.shape[1] + proj.shape[1]
    return pl.pallas_call(
        edges_kernel,
        in_specs=[anywhere()] * 2,
        out_specs=vmem(),
        out_shape=jax.ShapeDtypeStruct((EDGE, width), BF16),
        scratch_shapes=[pltpu.SemaphoreType.DMA((2,))],
        compiler_params=params(),
        name="edges",
    )(inner, proj)


def first_chunk(in_ref, head_ref, sem, first):
    return pltpu.make_async_copy(in_ref.at[pl.ds(0, CHUNK), pl.ds(first, head_ref.shape[1])], head_ref, sem)


def decay_kernel(decay_ref, step_ref, skip_ref, inner_ref, fwd_ref, inv_ref, dev_ref, fac_ref, head_ref, sem):
    head = first_chunk(inner_ref, head_ref, sem, 0)
    head.start()
    heads, rows = decay_ref.shape
    chunks = rows // CHUNK
    lower = jnp.where(iota((CHUNK, CHUNK), 0) >= iota((CHUNK, CHUNK), 1), 1.0, 0.0).astype(BF16)
    same = jnp.where(iota((CHUNK, CHUNK), 0) == iota((CHUNK, CHUNK), 1), 1.0, 0.0).astype(BF16)
    copies = LANES // heads
    cums, steps = [], []
    for c in range(chunks):
        at = pl.ds(c * CHUNK, CHUNK)
        decay = jnp.concatenate([decay_ref[:, at]] * copies, axis=0)
        step = jnp.concatenate([step_ref[:, at]] * copies, axis=0)
        cums.append(sum(dot_rows(lower, piece) for piece in pieces(decay, 3)))
        steps.append(sum(dot_rows(same, piece) for piece in pieces(step, 3)))
    totals = [cum[CHUNK - 1 :] for cum in cums]
    middles = [cum[CHUNK // 2 - 1 : CHUNK // 2] for cum in cums]
    before = [jnp.zeros_like(totals[0])]
    for c in range(chunks):
        before.append(before[c] + totals[c])
    fac_ref[...] = jnp.zeros_like(fac_ref)
    for c in range(chunks):
        at = pl.ds(c * CHUNK, CHUNK)
        fwd_ref[at, :] = jnp.exp(cums[c] - middles[c])
        inv_ref[at, :] = jnp.exp(middles[c] - cums[c]) * steps[c]
        dev_ref[at, :] = jnp.exp(before[c] + cums[c])
        following = middles[c + 1] if c + 1 < chunks else 0.0
        fac_ref[c : c + 1, :] = jnp.exp(totals[c] - middles[c] + following)
    fac_ref[chunks : chunks + 1, :] = skip_ref[:1]
    fac_ref[8:9, :] = jnp.exp(before[chunks])
    head.wait()


def decays(decay_log, step_size, skip_weight, inner):
    rows, heads = decay_log.shape
    wide = jax.ShapeDtypeStruct((rows, LANES), F32)
    return pl.pallas_call(
        decay_kernel,
        in_specs=[vmem()] * 3 + [anywhere()],
        out_specs=[vmem()] * 5,
        out_shape=(wide, wide, wide, jax.ShapeDtypeStruct((16, LANES), F32), jax.ShapeDtypeStruct((CHUNK, inner.shape[1] // GROUPS), BF16)),
        scratch_shapes=[pltpu.SemaphoreType.DMA],
        compiler_params=params(),
        name="decays",
    )(decay_log.T, step_size.T, jnp.broadcast_to(jnp.tile(skip_weight, LANES // heads)[None], (8, LANES)), inner)


def project(proj_ref, edge_ref, taps_ref, mix_ref, bt_ref, wide_ref):
    rows, width = proj_ref.shape
    state = width // 2
    taps = [taps_ref[k : k + 1, :] for k in range(taps_ref.shape[0])]
    causal = iota((CHUNK, CHUNK), 0) >= iota((CHUNK, CHUNK), 1)
    past = edge_ref.shape[0]
    wide_ref[EDGE - past : EDGE, :] = edge_ref[:, edge_ref.shape[1] - width :].astype(F32)
    wide_ref[EDGE:, :] = proj_ref[...].astype(F32)
    for c in range(rows // CHUNK):
        at = pl.ds(c * CHUNK, CHUNK)
        both = silu_conv(lambda k: wide_ref[pl.ds(EDGE + c * CHUNK - k, CHUNK), :], taps).astype(BF16)
        b_rows, c_rows = both[:, :state], both[:, state:]
        mix_ref[at, :CHUNK] = jnp.where(causal, dot_rows(c_rows, b_rows), 0.0).astype(BF16)
        mix_ref[at, CHUNK:] = c_rows
        bt_ref[:, at] = b_rows.astype(F32).T.astype(BF16)


def summarize(place_ref, in_ref, ready, edge_ref, taps_ref, inv_ref, fac_ref, bt_ref, x_ref, scaled_ref, opening_ref, slots, window_ref, sum_ref, row_ref, head_width, first):
    rows, wide = x_ref.shape
    cols = wide // SQUARE
    state = bt_ref.shape[0]
    count = taps_ref.shape[0]
    chunks = rows // CHUNK
    for block in range(wide // LANES):
        at_lanes = pl.ds(first + block * LANES, LANES)
        window_ref[block, EDGE + CHUNK - count + 1 :, :] = edge_ref[:, at_lanes].astype(F32)
    row_ref[...] = over_heads(fac_ref[...], head_width, first, wide)
    sum_ref[...] = jnp.zeros_like(sum_ref)

    def chunk_step(c, _):
        ready(c)
        at = pl.ds(pl.multiple_of(c * CHUNK, CHUNK), CHUNK)
        for sub in range(wide // SUB):
            at_cols = pl.ds(sub * SUB, SUB)
            here = first + sub * SUB
            rows_here = in_ref[at, at_cols].astype(F32)
            xs = []
            for lane in range(0, SUB, LANES):
                block = (sub * SUB + lane) // LANES
                window_ref[block, EDGE - 8 : EDGE, :] = window_ref[block, EDGE + CHUNK - 8 :, :]
                window_ref[block, EDGE:, :] = rows_here[:, lane : lane + LANES]
                taps = [taps_ref[k : k + 1, pl.ds(here + lane, LANES)] for k in range(count)]
                xs.append(silu_conv(lambda k: window_ref[block, pl.ds(EDGE - k, CHUNK), :], taps))
            x = jnp.concatenate(xs, axis=1)
            x_ref[at, at_cols] = x.astype(BF16)
            scaled = over_heads(inv_ref[at, :], head_width, here, SUB).astype(BF16) * x.astype(BF16)
            scaled_ref[at, at_cols] = scaled
            running = sum_ref[:, at_cols]
            opening_ref[at, at_cols] = running.astype(BF16)
            sum_ref[:, at_cols] = row_ref[pl.ds(c, 1), at_cols] * (running + dot(bt_ref[:, at], scaled))
        return 0

    lax.fori_loop(0, chunks, chunk_step, 0)
    row = iota((EDGE, cols), 0)
    for k, slot in enumerate(slots):
        start = pl.multiple_of((k ^ lax.rem(place_ref[0], SQUARE)) * cols, cols)
        slot[:state, :] = sum_ref[:, pl.ds(start, cols)].astype(BF16)
        decay = row_ref[8:16, pl.ds(start, cols)][:1]
        high = decay.astype(BF16).astype(F32)
        slot[state:, :] = jnp.where(row == 0, high, jnp.where(row == 1, decay - high, 0.0)).astype(BF16)


def first_kernel(place_ref, in_ref, head_ref, proj_ref, edge_ref, taps_ref, proj_taps_ref, inv_ref, fac_ref, x_ref, scaled_ref, opening_ref, mix_ref, bt_ref, next_ref, *rest, head_width):
    slots, (block_ref, wide_ref, window_ref, sum_ref, row_ref, sems) = rest[:SQUARE], rest[SQUARE:]
    rows, wide = x_ref.shape

    def fetch(c):
        at = pl.ds(pl.multiple_of(c * CHUNK, CHUNK), CHUNK)
        return pltpu.make_async_copy(in_ref.at[at, pl.ds(0, wide)], block_ref.at[at, :], sems.at[c])

    for c in range(1, rows // CHUNK):
        fetch(c).start()
    upcoming = first_chunk(in_ref, next_ref, sems.at[0], wide)
    upcoming.start()
    block_ref[:CHUNK, :] = head_ref[...]
    project(proj_ref, edge_ref, proj_taps_ref, mix_ref, bt_ref, wide_ref)
    summarize(place_ref, block_ref, lambda c: pl.when(c > 0)(lambda: fetch(c).wait()), edge_ref, taps_ref, inv_ref, fac_ref, bt_ref, x_ref, scaled_ref, opening_ref, slots, window_ref, sum_ref, row_ref, head_width, 0)
    upcoming.wait()


def slot_shapes(state, wide):
    return [jax.ShapeDtypeStruct((state + EDGE, wide // SQUARE), BF16)] * SQUARE


def sum_scratch(state, wide):
    return [pltpu.VMEM((wide // LANES, EDGE + CHUNK, LANES), F32), pltpu.VMEM((state, wide), F32), pltpu.VMEM((16, wide), F32)]


def first_states(place, inner, head, proj, edge, taps, proj_taps, inv, fac, head_width):
    rows, width = inner.shape
    state = proj.shape[1] // 2
    wide = width // GROUPS
    chunks = rows // CHUNK
    out = pl.pallas_call(
        lambda *refs: first_kernel(*refs, head_width=head_width),
        in_specs=[smem(), anywhere()] + [vmem()] * 7,
        out_specs=[vmem()] * (SQUARE + 6),
        out_shape=[
            jax.ShapeDtypeStruct((rows, wide), BF16),
            jax.ShapeDtypeStruct((rows, wide), BF16),
            jax.ShapeDtypeStruct((chunks * state, wide), BF16),
            jax.ShapeDtypeStruct((rows, CHUNK + state), BF16),
            jax.ShapeDtypeStruct((state, rows), BF16),
            jax.ShapeDtypeStruct((CHUNK, wide), BF16),
        ]
        + slot_shapes(state, wide),
        scratch_shapes=[pltpu.VMEM((rows, wide), BF16), pltpu.VMEM((EDGE + rows, 2 * state), F32)]
        + sum_scratch(state, wide)
        + [pltpu.SemaphoreType.DMA((chunks,))],
        compiler_params=params(),
        name="first_states",
    )(place, inner, head, proj, edge, taps, proj_taps, inv, fac)
    return out[:3], out[3:6], out[6:]


def later_kernel(place_ref, in_ref, head_ref, edge_ref, taps_ref, inv_ref, fac_ref, bt_ref, x_ref, scaled_ref, opening_ref, *rest, head_width, first):
    slots, (block_ref, window_ref, sum_ref, row_ref, sems) = rest[:SQUARE], rest[SQUARE:]
    rows, wide = x_ref.shape

    def fetch(c):
        at = pl.ds(pl.multiple_of(c * CHUNK, CHUNK), CHUNK)
        return pltpu.make_async_copy(in_ref.at[at, pl.ds(first, wide)], block_ref.at[at, :], sems.at[c])

    for c in range(1, rows // CHUNK):
        fetch(c).start()
    block_ref[:CHUNK, :] = head_ref[...]
    summarize(place_ref, block_ref, lambda c: pl.when(c > 0)(lambda: fetch(c).wait()), edge_ref, taps_ref, inv_ref, fac_ref, bt_ref, x_ref, scaled_ref, opening_ref, slots, window_ref, sum_ref, row_ref, head_width, first)


def later_states(place, inner, head, edge, taps, inv, fac, bt, head_width, group):
    rows, width = inner.shape
    wide = width // GROUPS
    state = bt.shape[0]
    chunks = rows // CHUNK
    out = pl.pallas_call(
        lambda *refs: later_kernel(*refs, head_width=head_width, first=group * wide),
        in_specs=[smem(), anywhere()] + [vmem()] * 6,
        out_specs=[vmem()] * (SQUARE + 3),
        out_shape=[
            jax.ShapeDtypeStruct((rows, wide), BF16),
            jax.ShapeDtypeStruct((rows, wide), BF16),
            jax.ShapeDtypeStruct((chunks * state, wide), BF16),
        ]
        + slot_shapes(state, wide),
        scratch_shapes=[pltpu.VMEM((rows, wide), BF16)] + sum_scratch(state, wide) + [pltpu.SemaphoreType.DMA((chunks,))],
        compiler_params=params(),
        name="later_states",
    )(place, inner, head, edge, taps, inv, fac, bt)
    return out[:3], out[3:]


def combine_kernel(place_ref, *refs):
    slots, (leaving_ref, prefix_ref, opening_ref, placed_ref) = refs[:SQUARE], refs[SQUARE:]
    state, cols = leaving_ref.shape
    spot = lax.rem(place_ref[0], SQUARE)
    for k in range(SQUARE):
        placed_ref[spot ^ k] = slots[k][...]
    running = jnp.zeros((state, cols), F32)
    opening = jnp.ones((1, cols), F32)
    begun = jnp.where(place_ref[0] < SQUARE, 0.0, 1.0)
    for p in range(SQUARE):
        prefix_ref[spot ^ p] = running
        opening_ref[spot ^ p] = jnp.broadcast_to(begun * opening, (8, cols))
        tail = placed_ref[p, state:, :].astype(F32)
        decay = tail[0:1] + tail[1:2]
        running = decay * running + placed_ref[p, :state, :].astype(F32)
        opening = decay * opening
    leaving_ref[...] = running.astype(BF16)
    opening_ref[SQUARE] = jnp.broadcast_to(opening, (8, cols))


def combine(place, slots):
    rows, cols = slots[0].shape
    state = rows - EDGE
    return pl.pallas_call(
        combine_kernel,
        in_specs=[smem()] + [vmem()] * SQUARE,
        out_specs=[vmem()] * 3,
        out_shape=(
            jax.ShapeDtypeStruct((state, cols), BF16),
            jax.ShapeDtypeStruct((SQUARE, state, cols), F32),
            jax.ShapeDtypeStruct((SQUARE + 1, 8, cols), F32),
        ),
        scratch_shapes=[pltpu.VMEM((SQUARE, rows, cols), BF16)],
        compiler_params=params(),
        name="combine",
    )(place, *slots)


def local_kernel(x_ref, scaled_ref, opening_ref, fwd_ref, fac_ref, mix_ref, out_ref, *, head_width, first):
    rows, wide = x_ref.shape
    chunks = rows // CHUNK
    state = opening_ref.shape[0] // chunks
    cols = wide // SQUARE

    def tile_step(j, _):
        base = pl.multiple_of(j * cols, cols)
        at_cols = pl.ds(base, cols)
        skip = over_heads(fac_ref[...], head_width, first + base, cols)[chunks : chunks + 1]
        for c in range(chunks):
            at = pl.ds(c * CHUNK, CHUNK)
            both = jnp.concatenate([scaled_ref[at, at_cols], opening_ref[pl.ds(c * state, state), at_cols]], axis=0)
            mixed = over_heads(fwd_ref[at, :], head_width, first + base, cols) * dot(mix_ref[at, :], both)
            out_ref[at, at_cols] = mixed + skip * x_ref[at, at_cols].astype(F32)
        return 0

    lax.fori_loop(0, SQUARE, tile_step, 0)


def local_parts(x, scaled, opening, fwd, fac, mix, head_width, group):
    rows, wide = x.shape
    return pl.pallas_call(
        lambda *refs: local_kernel(*refs, head_width=head_width, first=group * wide),
        in_specs=[vmem()] * 6,
        out_specs=vmem(),
        out_shape=jax.ShapeDtypeStruct((rows, wide), F32),
        compiler_params=params(),
        name="local",
    )(x, scaled, opening, fwd, fac, mix)


def normalize(place_ref, local_ref, dev_ref, mix_ref, gain_ref, slots, head_width, first, done):
    rows, wide = local_ref.shape
    cols = wide // SQUARE
    mean = jnp.where(iota((SUB, SUB), 0) // head_width == iota((SUB, SUB), 1) // head_width, 1.0 / head_width, 0.0).astype(BF16)
    for k in range(SQUARE):
        base = pl.multiple_of((k ^ lax.rem(place_ref[0], SQUARE)) * cols, cols)
        for sub in range(cols // SUB):
            at_cols = pl.ds(base + sub * SUB, SUB)
            here = first + base + sub * SUB
            carried = dot(mix_ref[:, CHUNK:], slots[k][:, sub * SUB : (sub + 1) * SUB])
            combined = local_ref[:, at_cols] + over_heads(dev_ref[...], head_width, here, SUB) * carried
            squares = dot((combined * combined).astype(BF16), mean)
            result = combined * lax.rsqrt(squares + 1e-05) * gain_ref[:, pl.ds(here, SUB)]
            done(k * (cols // SUB) + sub, base + sub * SUB, result.astype(BF16))


def finish_first_kernel(place_ref, local_ref, dev_ref, mix_ref, gain_ref, *rest, head_width):
    slots, out_ref = rest[:SQUARE], rest[SQUARE]

    def done(turn, column, result):
        out_ref[:, pl.ds(column, SUB)] = result

    normalize(place_ref, local_ref, dev_ref, mix_ref, gain_ref, slots, head_width, 0, done)


def finish_first(place, local, dev, mix, gain, slots, head_width):
    rows, wide = local.shape
    return pl.pallas_call(
        lambda *refs: finish_first_kernel(*refs, head_width=head_width),
        in_specs=[smem()] + [vmem()] * (4 + SQUARE),
        out_specs=vmem(),
        out_shape=jax.ShapeDtypeStruct((rows, wide), BF16),
        compiler_params=params(),
        name="finish_first",
    )(place, local, dev, mix, gain, *slots)


def finish_kernel(place_ref, local_ref, dev_ref, mix_ref, gain_ref, *rest, head_width):
    slots, (earlier_ref, out_ref, stage_ref, sems, earlier_sem) = rest[:SQUARE], rest[SQUARE:]
    first = earlier_ref.shape[1]
    earlier = pltpu.make_async_copy(earlier_ref, out_ref.at[:, pl.ds(0, first)], earlier_sem)
    earlier.start()
    copies = []

    def done(turn, column, result):
        stage_ref[turn] = result
        copies.append(pltpu.make_async_copy(stage_ref.at[turn], out_ref.at[:, pl.ds(first + column, SUB)], sems.at[turn]))
        copies[-1].start()

    normalize(place_ref, local_ref, dev_ref, mix_ref, gain_ref, slots, head_width, first, done)
    earlier.wait()
    for copy in copies:
        copy.wait()


def finish(place, local, dev, mix, gain, slots, earlier, head_width):
    rows, wide = local.shape
    return pl.pallas_call(
        lambda *refs: finish_kernel(*refs, head_width=head_width),
        in_specs=[smem()] + [vmem()] * (5 + SQUARE),
        out_specs=anywhere(),
        out_shape=jax.ShapeDtypeStruct((rows, wide * GROUPS), BF16),
        scratch_shapes=[pltpu.VMEM((wide // SUB, rows, SUB), BF16), pltpu.SemaphoreType.DMA((wide // SUB,)), pltpu.SemaphoreType.DMA],
        compiler_params=params(),
        name="finish",
    )(place, local, dev, mix, gain, *slots, earlier)


def shifted(x, by):
    length = lax.axis_size("ctx")
    return lax.ppermute(x, "ctx", [(i, i + by) for i in range(length - by)])


def swapped(x, k):
    length = lax.axis_size("ctx")
    return lax.ppermute(x, "ctx", [(i, i ^ k) for i in range(length)])


def previous_squares(leaving, decay):
    length = lax.axis_size("ctx")
    squares = length // SQUARE
    entering = lax.ppermute(leaving, "ctx", [(i, (i + SQUARE) % length) for i in range(length)])
    span = 1
    if squares > 2:
        entering = jnp.where(lax.axis_index("ctx") < SQUARE, jnp.zeros_like(entering), entering)
        window = shifted(decay, SQUARE)
    while span < squares - 1:
        behind = shifted(entering, SQUARE * span)
        entering = (entering.astype(F32) + window * behind.astype(F32)).astype(BF16)
        window = window * shifted(window, SQUARE * span)
        span *= 2
    return entering


def body(inner_input, state_proj, step_size, decay_log, conv_inner, conv_proj, skip_weight, norm_gain):
    rows, width = inner_input.shape
    heads = step_size.shape[1]
    head_width = width // heads
    past = conv_inner.shape[0] - 1
    kept, kept_proj = [pltpu.with_memory_space_constraint(a, pltpu.HBM) for a in (inner_input, state_proj)]
    place = jnp.full((1,), lax.axis_index("ctx"), jnp.int32)
    edge = shifted(last_rows(kept, kept_proj)[EDGE - past :], 1)
    fwd, inv, dev, fac, head = decays(decay_log, step_size, skip_weight, kept)
    gain = norm_gain[None]
    made, sent = [], []
    parts, (mix, bt, head), slots = first_states(place, kept, head, state_proj, edge, conv_inner, conv_proj, inv, fac, head_width)
    made.append(parts)
    sent.append([slots[0]] + [swapped(slots[k], k) for k in range(1, SQUARE)])
    parts, slots = later_states(place, kept, head, edge, conv_inner, inv, fac, bt, head_width, 1)
    made.append(parts)
    sent.append([slots[0]] + [swapped(slots[k], k) for k in range(1, SQUARE)])
    combined = [combine(place, sent[group]) for group in range(GROUPS)]
    arrived = [previous_squares(leaving, opening[SQUARE, :1]) for leaving, _, opening in combined]
    locals_ = [local_parts(*made[group], fwd, fac, mix, head_width, group) for group in range(GROUPS)]
    arrived[0], locals_[0] = lax.optimization_barrier((arrived[0], locals_[0]))
    returned = []
    for group in range(GROUPS):
        _, prefix, opening = combined[group]
        entering = [(prefix[k] + opening[k, :1] * arrived[group].astype(F32)).astype(BF16) for k in range(SQUARE)]
        returned.append([entering[0]] + [swapped(entering[k], k) for k in range(1, SQUARE)])
    earlier = finish_first(place, locals_[0], dev, mix, gain, returned[0], head_width)
    return finish(place, locals_[1], dev, mix, gain, returned[1], earlier, head_width)


def solution(mesh):
    split = P(("dp", "ctx"), None)
    return jax.shard_map(
        body, mesh=mesh, in_specs=(split, split, split, split, P(), P(), P(), P()), out_specs=split, check_vma=False
    )
```

```python
import jax
import jax.numpy as jnp
from jax import lax
from jax.experimental import pallas as pl
from jax.experimental.pallas import tpu as pltpu
from jax.sharding import PartitionSpec as P

CHUNK = 128
SQUARE = 4
GROUPS = 2
SUB = 256
EDGE = 16
LANES = 128
F32 = jnp.float32
BF16 = jnp.bfloat16


def params(mib=9):
    return pltpu.CompilerParams(vmem_limit_bytes=mib * 1024 * 1024)


def dot(a, b):
    return jnp.dot(a, b, preferred_element_type=F32)


def dot_rows(a, b):
    return lax.dot_general(a, b, (((1,), (1,)), ((), ())), preferred_element_type=F32)


def pieces(value, count):
    out = []
    for _ in range(count):
        out.append(value.astype(BF16))
        value = value - out[-1].astype(F32)
    return out


def iota(shape, axis):
    return lax.broadcasted_iota(jnp.int32, shape, axis)


def hint(moved):
    return pl.CostEstimate(flops=0, bytes_accessed=moved, transcendentals=0)


def vmem():
    return pl.BlockSpec(memory_space=pltpu.VMEM)


def smem():
    return pl.BlockSpec(memory_space=pltpu.SMEM)


def anywhere():
    return pl.BlockSpec(memory_space=pl.ANY)


def over_heads(values, head_width, first, cols):
    blocks = []
    for lane in range(0, cols, LANES):
        head = (first + lane + iota(values.shape, 1)) // head_width
        blocks.append(jnp.take_along_axis(values, head, axis=1, mode="promise_in_bounds"))
    return jnp.concatenate(blocks, axis=1)


def silu_conv(rows_back, taps):
    count = len(taps)
    half = sum(rows_back(k) * taps[count - 1 - k] for k in range(count))
    return half + half * jnp.tanh(half)


def first_chunk(in_ref, head_ref, sem, first):
    return pltpu.make_async_copy(in_ref.at[pl.ds(0, CHUNK), pl.ds(first, head_ref.shape[1])], head_ref, sem)


def edges_kernel(inner_ref, proj_ref, out_ref, head_ref, sems):
    width = inner_ref.shape[1]
    last = pl.ds(inner_ref.shape[0] - EDGE, EDGE)
    copies = [
        pltpu.make_async_copy(inner_ref.at[last, :], out_ref.at[:, :width], sems.at[0]),
        pltpu.make_async_copy(proj_ref.at[last, :], out_ref.at[:, width:], sems.at[1]),
        first_chunk(inner_ref, head_ref, sems.at[2], 0),
    ]
    for copy in copies:
        copy.start()
    for copy in copies:
        copy.wait()


def last_rows(inner, proj):
    width = inner.shape[1] + proj.shape[1]
    return pl.pallas_call(
        edges_kernel,
        in_specs=[anywhere()] * 2,
        out_specs=[vmem()] * 2,
        out_shape=[jax.ShapeDtypeStruct((EDGE, width), BF16), jax.ShapeDtypeStruct((CHUNK, inner.shape[1] // GROUPS), BF16)],
        scratch_shapes=[pltpu.SemaphoreType.DMA((3,))],
        compiler_params=params(),
        name="edges",
    )(inner, proj)


def decay_kernel(decay_ref, step_ref, skip_ref, fwd_ref, inv_ref, dev_ref, fac_ref):
    heads, rows = decay_ref.shape
    chunks = rows // CHUNK
    lower = jnp.where(iota((CHUNK, CHUNK), 0) >= iota((CHUNK, CHUNK), 1), 1.0, 0.0).astype(BF16)
    same = jnp.where(iota((CHUNK, CHUNK), 0) == iota((CHUNK, CHUNK), 1), 1.0, 0.0).astype(BF16)
    copies = LANES // heads
    cums, steps = [], []
    for c in range(chunks):
        at = pl.ds(c * CHUNK, CHUNK)
        decay = jnp.concatenate([decay_ref[:, at]] * copies, axis=0)
        step = jnp.concatenate([step_ref[:, at]] * copies, axis=0)
        cums.append(sum(dot_rows(lower, piece) for piece in pieces(decay, 3)))
        steps.append(sum(dot_rows(same, piece) for piece in pieces(step, 3)))
    totals = [cum[CHUNK - 1 :] for cum in cums]
    middles = [cum[CHUNK // 2 - 1 : CHUNK // 2] for cum in cums]
    before = [jnp.zeros_like(totals[0])]
    for c in range(chunks):
        before.append(before[c] + totals[c])
    fac_ref[...] = jnp.zeros_like(fac_ref)
    for c in range(chunks):
        at = pl.ds(c * CHUNK, CHUNK)
        fwd_ref[at, :] = jnp.exp(cums[c] - middles[c])
        inv_ref[at, :] = jnp.exp(middles[c] - cums[c]) * steps[c]
        dev_ref[at, :] = jnp.exp(before[c] + cums[c])
        following = middles[c + 1] if c + 1 < chunks else 0.0
        fac_ref[c : c + 1, :] = jnp.exp(totals[c] - middles[c] + following)
    fac_ref[chunks : chunks + 1, :] = skip_ref[:1]
    fac_ref[8:9, :] = jnp.exp(before[chunks])


def decays(decay_log, step_size, skip_weight):
    rows, heads = decay_log.shape
    wide = jax.ShapeDtypeStruct((rows, LANES), F32)
    return pl.pallas_call(
        decay_kernel,
        out_shape=(wide, wide, wide, jax.ShapeDtypeStruct((16, LANES), F32)),
        compiler_params=params(),
        name="decays",
    )(decay_log.T, step_size.T, jnp.broadcast_to(jnp.tile(skip_weight, LANES // heads)[None], (8, LANES)))


def project(proj_ref, edge_ref, taps_ref, mix_ref, bt_ref, wide_ref):
    rows, width = proj_ref.shape
    state = width // 2
    taps = [0.5 * taps_ref[k : k + 1, :] for k in range(taps_ref.shape[0])]
    causal = iota((CHUNK, CHUNK), 0) >= iota((CHUNK, CHUNK), 1)
    past = edge_ref.shape[0]
    wide_ref[EDGE - past : EDGE, :] = edge_ref[:, edge_ref.shape[1] - width :].astype(F32)
    wide_ref[EDGE:, :] = proj_ref[...].astype(F32)
    for c in range(rows // CHUNK):
        at = pl.ds(c * CHUNK, CHUNK)
        both = silu_conv(lambda k: wide_ref[pl.ds(EDGE + c * CHUNK - k, CHUNK), :], taps).astype(BF16)
        b_rows, c_rows = both[:, :state], both[:, state:]
        mix_ref[at, :CHUNK] = jnp.where(causal, dot_rows(c_rows, b_rows), 0.0).astype(BF16)
        mix_ref[at, CHUNK:] = c_rows
        bt_ref[:, at] = b_rows.astype(F32).T.astype(BF16)


def summarize(place_ref, in_ref, ready, edge_ref, taps_ref, inv_ref, fac_ref, bt_ref, x_ref, scaled_ref, opening_ref, slots, window_ref, sum_ref, row_ref, half_ref, head_width, first):
    rows, wide = x_ref.shape
    cols = wide // SQUARE
    state = bt_ref.shape[0]
    count = taps_ref.shape[0]
    chunks = rows // CHUNK
    for block in range(wide // LANES):
        at_lanes = pl.ds(first + block * LANES, LANES)
        window_ref[block, EDGE + CHUNK - count + 1 :, :] = edge_ref[:, at_lanes].astype(F32)
        half_ref[block] = 0.5 * taps_ref[:, at_lanes]
    row_ref[...] = over_heads(fac_ref[...], head_width, first, wide)
    sum_ref[...] = jnp.zeros_like(sum_ref)

    def chunk_step(c, _):
        ready(c)
        at = pl.ds(pl.multiple_of(c * CHUNK, CHUNK), CHUNK)
        for sub in range(wide // SUB):
            at_cols = pl.ds(sub * SUB, SUB)
            here = first + sub * SUB
            rows_here = in_ref[at, at_cols].astype(F32)
            xs = []
            for lane in range(0, SUB, LANES):
                block = (sub * SUB + lane) // LANES
                window_ref[block, EDGE - 8 : EDGE, :] = window_ref[block, EDGE + CHUNK - 8 :, :]
                window_ref[block, EDGE:, :] = rows_here[:, lane : lane + LANES]
                taps = [half_ref[block, k : k + 1, :] for k in range(count)]
                xs.append(silu_conv(lambda k: window_ref[block, pl.ds(EDGE - k, CHUNK), :], taps))
            x = jnp.concatenate(xs, axis=1)
            x_ref[at, at_cols] = x.astype(BF16)
            scaled = over_heads(inv_ref[at, :], head_width, here, SUB).astype(BF16) * x.astype(BF16)
            scaled_ref[at, at_cols] = scaled
            running = sum_ref[:, at_cols]
            opening_ref[at, at_cols] = running.astype(BF16)
            sum_ref[:, at_cols] = row_ref[pl.ds(c, 1), at_cols] * (running + dot(bt_ref[:, at], scaled))
        return 0

    lax.fori_loop(0, chunks, chunk_step, 0)
    row = iota((EDGE, cols), 0)
    for k, slot in enumerate(slots):
        start = pl.multiple_of((k ^ lax.rem(place_ref[0], SQUARE)) * cols, cols)
        slot[:state, :] = sum_ref[:, pl.ds(start, cols)].astype(BF16)
        decay = row_ref[8:16, pl.ds(start, cols)][:1]
        high = decay.astype(BF16).astype(F32)
        slot[state:, :] = jnp.where(row == 0, high, jnp.where(row == 1, decay - high, 0.0)).astype(BF16)


def first_kernel(place_ref, in_ref, head_ref, proj_ref, edge_ref, taps_ref, proj_taps_ref, inv_ref, fac_ref, x_ref, scaled_ref, opening_ref, mix_ref, bt_ref, next_ref, *rest, head_width):
    slots, (block_ref, wide_ref, window_ref, sum_ref, row_ref, half_ref, sems) = rest[:SQUARE], rest[SQUARE:]
    rows, wide = x_ref.shape

    def fetch(c):
        at = pl.ds(pl.multiple_of(c * CHUNK, CHUNK), CHUNK)
        return pltpu.make_async_copy(in_ref.at[at, pl.ds(0, wide)], block_ref.at[at, :], sems.at[c])

    for c in range(1, rows // CHUNK):
        fetch(c).start()
    upcoming = first_chunk(in_ref, next_ref, sems.at[0], wide)
    upcoming.start()
    block_ref[:CHUNK, :] = head_ref[...]
    project(proj_ref, edge_ref, proj_taps_ref, mix_ref, bt_ref, wide_ref)
    summarize(place_ref, block_ref, lambda c: pl.when(c > 0)(lambda: fetch(c).wait()), edge_ref, taps_ref, inv_ref, fac_ref, bt_ref, x_ref, scaled_ref, opening_ref, slots, window_ref, sum_ref, row_ref, half_ref, head_width, 0)
    upcoming.wait()


def slot_shapes(state, wide):
    return [jax.ShapeDtypeStruct((state + EDGE, wide // SQUARE), BF16)] * SQUARE


def sum_scratch(state, wide, taps):
    return [pltpu.VMEM((wide // LANES, EDGE + CHUNK, LANES), F32), pltpu.VMEM((state, wide), F32), pltpu.VMEM((16, wide), F32), pltpu.VMEM((wide // LANES, taps, LANES), F32)]


def first_states(place, inner, head, proj, edge, taps, proj_taps, inv, fac, head_width):
    rows, width = inner.shape
    state = proj.shape[1] // 2
    wide = width // GROUPS
    chunks = rows // CHUNK
    out = pl.pallas_call(
        lambda *refs: first_kernel(*refs, head_width=head_width),
        in_specs=[smem(), anywhere()] + [vmem()] * 7,
        out_specs=[vmem()] * (SQUARE + 6),
        out_shape=[
            jax.ShapeDtypeStruct((rows, wide), BF16),
            jax.ShapeDtypeStruct((rows, wide), BF16),
            jax.ShapeDtypeStruct((chunks * state, wide), BF16),
            jax.ShapeDtypeStruct((rows, CHUNK + state), BF16),
            jax.ShapeDtypeStruct((state, rows), BF16),
            jax.ShapeDtypeStruct((CHUNK, wide), BF16),
        ]
        + slot_shapes(state, wide),
        scratch_shapes=[pltpu.VMEM((rows, wide), BF16), pltpu.VMEM((EDGE + rows, 2 * state), F32)]
        + sum_scratch(state, wide, taps.shape[0])
        + [pltpu.SemaphoreType.DMA((chunks,))],
        compiler_params=params(),
        name="first_states",
    )(place, inner, head, proj, edge, taps, proj_taps, inv, fac)
    return out[:3], out[3:6], out[6:]


def later_kernel(place_ref, in_ref, head_ref, edge_ref, taps_ref, inv_ref, fac_ref, bt_ref, x_ref, scaled_ref, opening_ref, *rest, head_width, first):
    slots, (block_ref, window_ref, sum_ref, row_ref, half_ref, sems) = rest[:SQUARE], rest[SQUARE:]
    rows, wide = x_ref.shape

    def fetch(c):
        at = pl.ds(pl.multiple_of(c * CHUNK, CHUNK), CHUNK)
        return pltpu.make_async_copy(in_ref.at[at, pl.ds(first, wide)], block_ref.at[at, :], sems.at[c])

    for c in range(1, rows // CHUNK):
        fetch(c).start()
    block_ref[:CHUNK, :] = head_ref[...]
    summarize(place_ref, block_ref, lambda c: pl.when(c > 0)(lambda: fetch(c).wait()), edge_ref, taps_ref, inv_ref, fac_ref, bt_ref, x_ref, scaled_ref, opening_ref, slots, window_ref, sum_ref, row_ref, half_ref, head_width, first)


def later_states(place, inner, head, edge, taps, inv, fac, bt, head_width, group):
    rows, width = inner.shape
    wide = width // GROUPS
    state = bt.shape[0]
    chunks = rows // CHUNK
    out = pl.pallas_call(
        lambda *refs: later_kernel(*refs, head_width=head_width, first=group * wide),
        in_specs=[smem(), anywhere()] + [vmem()] * 6,
        out_specs=[vmem()] * (SQUARE + 3),
        out_shape=[
            jax.ShapeDtypeStruct((rows, wide), BF16),
            jax.ShapeDtypeStruct((rows, wide), BF16),
            jax.ShapeDtypeStruct((chunks * state, wide), BF16),
        ]
        + slot_shapes(state, wide),
        scratch_shapes=[pltpu.VMEM((rows, wide), BF16)] + sum_scratch(state, wide, taps.shape[0]) + [pltpu.SemaphoreType.DMA((chunks,))],
        compiler_params=params(),
        name="later_states",
    )(place, inner, head, edge, taps, inv, fac, bt)
    return out[:3], out[3:]


def combine_kernel(place_ref, *refs):
    slots, (leaving_ref, prefix_ref, opening_ref, placed_ref) = refs[:SQUARE], refs[SQUARE:]
    state, cols = leaving_ref.shape
    spot = lax.rem(place_ref[0], SQUARE)
    for k in range(SQUARE):
        placed_ref[spot ^ k] = slots[k][...]
    running = jnp.zeros((state, cols), F32)
    opening = jnp.ones((1, cols), F32)
    begun = jnp.where(place_ref[0] < SQUARE, 0.0, 1.0)
    for p in range(SQUARE):
        prefix_ref[spot ^ p] = running
        opening_ref[spot ^ p] = jnp.broadcast_to(begun * opening, (8, cols))
        tail = placed_ref[p, state:, :].astype(F32)
        decay = tail[0:1] + tail[1:2]
        running = decay * running + placed_ref[p, :state, :].astype(F32)
        opening = decay * opening
    leaving_ref[...] = running.astype(BF16)
    opening_ref[SQUARE] = jnp.broadcast_to(opening, (8, cols))


def combine(place, slots):
    rows, cols = slots[0].shape
    state = rows - EDGE
    return pl.pallas_call(
        combine_kernel,
        in_specs=[smem()] + [vmem()] * SQUARE,
        out_specs=[vmem()] * 3,
        out_shape=(
            jax.ShapeDtypeStruct((state, cols), BF16),
            jax.ShapeDtypeStruct((SQUARE, state, cols), F32),
            jax.ShapeDtypeStruct((SQUARE + 1, 8, cols), F32),
        ),
        scratch_shapes=[pltpu.VMEM((SQUARE, rows, cols), BF16)],
        compiler_params=params(),
        name="combine",
    )(place, *slots)


def local_kernel(x_ref, scaled_ref, opening_ref, fwd_ref, fac_ref, mix_ref, out_ref, *, head_width, first):
    rows, wide = x_ref.shape
    chunks = rows // CHUNK
    state = opening_ref.shape[0] // chunks
    cols = wide // SQUARE

    def tile_step(j, _):
        base = pl.multiple_of(j * cols, cols)
        at_cols = pl.ds(base, cols)
        skip = over_heads(fac_ref[...], head_width, first + base, cols)[chunks : chunks + 1]
        for c in range(chunks):
            at = pl.ds(c * CHUNK, CHUNK)
            both = jnp.concatenate([scaled_ref[at, at_cols], opening_ref[pl.ds(c * state, state), at_cols]], axis=0)
            mixed = over_heads(fwd_ref[at, :], head_width, first + base, cols) * dot(mix_ref[at, :], both)
            out_ref[at, at_cols] = mixed + skip * x_ref[at, at_cols].astype(F32)
        return 0

    lax.fori_loop(0, SQUARE, tile_step, 0, unroll=2)


def local_parts(x, scaled, opening, fwd, fac, mix, head_width, group):
    rows, wide = x.shape
    return pl.pallas_call(
        lambda *refs: local_kernel(*refs, head_width=head_width, first=group * wide),
        in_specs=[vmem()] * 6,
        out_specs=vmem(),
        out_shape=jax.ShapeDtypeStruct((rows, wide), F32),
        compiler_params=params(),
        name="local",
    )(x, scaled, opening, fwd, fac, mix)


def normalize(place_ref, local_ref, dev_ref, mix_ref, gain_ref, slots, head_width, first, done):
    rows, wide = local_ref.shape
    cols = wide // SQUARE
    mean = jnp.where(iota((SUB, SUB), 0) // head_width == iota((SUB, SUB), 1) // head_width, 1.0 / head_width, 0.0).astype(BF16)
    for k in range(SQUARE):
        base = pl.multiple_of((k ^ lax.rem(place_ref[0], SQUARE)) * cols, cols)
        for sub in range(cols // SUB):
            at_cols = pl.ds(base + sub * SUB, SUB)
            here = first + base + sub * SUB
            carried = dot(mix_ref[:, CHUNK:], slots[k][:, sub * SUB : (sub + 1) * SUB])
            combined = local_ref[:, at_cols] + over_heads(dev_ref[...], head_width, here, SUB) * carried
            squares = dot((combined * combined).astype(BF16), mean)
            result = combined * lax.rsqrt(squares + 1e-05) * gain_ref[:, pl.ds(here, SUB)]
            done(k * (cols // SUB) + sub, base + sub * SUB, result.astype(BF16))


def finish_first_kernel(place_ref, local_ref, dev_ref, mix_ref, gain_ref, *rest, head_width):
    slots, out_ref = rest[:SQUARE], rest[SQUARE]

    def done(turn, column, result):
        out_ref[:, pl.ds(column, SUB)] = result

    normalize(place_ref, local_ref, dev_ref, mix_ref, gain_ref, slots, head_width, 0, done)


def finish_first(place, local, dev, mix, gain, slots, head_width):
    rows, wide = local.shape
    return pl.pallas_call(
        lambda *refs: finish_first_kernel(*refs, head_width=head_width),
        in_specs=[smem()] + [vmem()] * (4 + SQUARE),
        out_specs=vmem(),
        out_shape=jax.ShapeDtypeStruct((rows, wide), BF16),
        compiler_params=params(),
        name="finish_first",
    )(place, local, dev, mix, gain, *slots)


def finish_kernel(place_ref, local_ref, dev_ref, mix_ref, gain_ref, *rest, head_width):
    slots, (earlier_ref, out_ref, stage_ref, sems, earlier_sem) = rest[:SQUARE], rest[SQUARE:]
    first = earlier_ref.shape[1]
    earlier = pltpu.make_async_copy(earlier_ref, out_ref.at[:, pl.ds(0, first)], earlier_sem)
    earlier.start()
    copies = []

    def done(turn, column, result):
        stage_ref[turn] = result
        copies.append(pltpu.make_async_copy(stage_ref.at[turn], out_ref.at[:, pl.ds(first + column, SUB)], sems.at[turn]))
        copies[-1].start()

    normalize(place_ref, local_ref, dev_ref, mix_ref, gain_ref, slots, head_width, first, done)
    earlier.wait()
    for copy in copies:
        copy.wait()


def finish(place, local, dev, mix, gain, slots, earlier, head_width):
    rows, wide = local.shape
    return pl.pallas_call(
        lambda *refs: finish_kernel(*refs, head_width=head_width),
        in_specs=[smem()] + [vmem()] * (5 + SQUARE),
        out_specs=anywhere(),
        out_shape=jax.ShapeDtypeStruct((rows, wide * GROUPS), BF16),
        scratch_shapes=[pltpu.VMEM((wide // SUB, rows, SUB), BF16), pltpu.SemaphoreType.DMA((wide // SUB,)), pltpu.SemaphoreType.DMA],
        compiler_params=params(),
        name="finish",
    )(place, local, dev, mix, gain, *slots, earlier)


def shifted(x, by):
    length = lax.axis_size("ctx")
    return lax.ppermute(x, "ctx", [(i, i + by) for i in range(length - by)])


def swapped(x, k):
    length = lax.axis_size("ctx")
    return lax.ppermute(x, "ctx", [(i, i ^ k) for i in range(length)])


def previous_squares(leaving, decay):
    length = lax.axis_size("ctx")
    squares = length // SQUARE
    entering = lax.ppermute(leaving, "ctx", [(i, (i + SQUARE) % length) for i in range(length)])
    span = 1
    if squares > 2:
        entering = jnp.where(lax.axis_index("ctx") < SQUARE, jnp.zeros_like(entering), entering)
        window = shifted(decay, SQUARE)
    while span < squares - 1:
        behind = shifted(entering, SQUARE * span)
        entering = (entering.astype(F32) + window * behind.astype(F32)).astype(BF16)
        window = window * shifted(window, SQUARE * span)
        span *= 2
    return entering


def body(inner_input, state_proj, step_size, decay_log, conv_inner, conv_proj, skip_weight, norm_gain):
    rows, width = inner_input.shape
    heads = step_size.shape[1]
    head_width = width // heads
    past = conv_inner.shape[0] - 1
    kept, kept_proj = [pltpu.with_memory_space_constraint(a, pltpu.HBM) for a in (inner_input, state_proj)]
    place = jnp.full((1,), lax.axis_index("ctx"), jnp.int32)
    edge, head = last_rows(kept, kept_proj)
    edge = shifted(edge[EDGE - past :], 1)
    fwd, inv, dev, fac = decays(decay_log, step_size, skip_weight)
    gain = norm_gain[None]
    made, sent = [], []
    parts, (mix, bt, head), slots = first_states(place, kept, head, state_proj, edge, conv_inner, conv_proj, inv, fac, head_width)
    made.append(parts)
    sent.append([slots[0]] + [swapped(slots[k], k) for k in range(1, SQUARE)])
    parts, slots = later_states(place, kept, head, edge, conv_inner, inv, fac, bt, head_width, 1)
    made.append(parts)
    sent.append([slots[0]] + [swapped(slots[k], k) for k in range(1, SQUARE)])
    made[0], sent[0] = lax.optimization_barrier((made[0], sent[0]))
    combined = [combine(place, sent[group]) for group in range(GROUPS)]
    arrived = [previous_squares(leaving, opening[SQUARE, :1]) for leaving, _, opening in combined]
    locals_ = [local_parts(*made[group], fwd, fac, mix, head_width, group) for group in range(GROUPS)]
    arrived[0], locals_[0] = lax.optimization_barrier((arrived[0], locals_[0]))
    returned = []
    for group in range(GROUPS):
        _, prefix, opening = combined[group]
        entering = [(prefix[k] + opening[k, :1] * arrived[group].astype(F32)).astype(BF16) for k in range(SQUARE)]
        returned.append([entering[0]] + [swapped(entering[k], k) for k in range(1, SQUARE)])
    earlier = finish_first(place, locals_[0], dev, mix, gain, returned[0], head_width)
    return finish(place, locals_[1], dev, mix, gain, returned[1], earlier, head_width)


def solution(mesh):
    split = P(("dp", "ctx"), None)
    return jax.shard_map(
        body, mesh=mesh, in_specs=(split, split, split, split, P(), P(), P(), P()), out_specs=split, check_vma=False
    )
```

```python
import jax
import jax.numpy as jnp
from jax import lax
from jax.experimental import pallas as pl
from jax.experimental.pallas import tpu as pltpu
from jax.sharding import PartitionSpec as P

CHUNK = 128
SQUARE = 4
GROUPS = 2
SUB = 256
EDGE = 16
LANES = 128
F32 = jnp.float32
BF16 = jnp.bfloat16


def params(mib=9):
    return pltpu.CompilerParams(vmem_limit_bytes=mib * 1024 * 1024)


def dot(a, b):
    return jnp.dot(a, b, preferred_element_type=F32)


def dot_rows(a, b):
    return lax.dot_general(a, b, (((1,), (1,)), ((), ())), preferred_element_type=F32)


def pieces(value, count):
    out = []
    for _ in range(count):
        out.append(value.astype(BF16))
        value = value - out[-1].astype(F32)
    return out


def iota(shape, axis):
    return lax.broadcasted_iota(jnp.int32, shape, axis)


def hint(moved):
    return pl.CostEstimate(flops=0, bytes_accessed=moved, transcendentals=0)


def vmem():
    return pl.BlockSpec(memory_space=pltpu.VMEM)


def smem():
    return pl.BlockSpec(memory_space=pltpu.SMEM)


def anywhere():
    return pl.BlockSpec(memory_space=pl.ANY)


def over_heads(values, head_width, first, cols):
    blocks = []
    for lane in range(0, cols, LANES):
        head = (first + lane + iota(values.shape, 1)) // head_width
        blocks.append(jnp.take_along_axis(values, head, axis=1, mode="promise_in_bounds"))
    return jnp.concatenate(blocks, axis=1)


def silu_conv(rows_back, taps):
    count = len(taps)
    half = sum(rows_back(k) * taps[count - 1 - k] for k in range(count))
    return half + half * jnp.tanh(half)


def first_chunk(in_ref, head_ref, sem, first):
    return pltpu.make_async_copy(in_ref.at[pl.ds(0, CHUNK), pl.ds(first, head_ref.shape[1])], head_ref, sem)


def edges_kernel(inner_ref, proj_ref, out_ref, head_ref, sems):
    width = inner_ref.shape[1]
    last = pl.ds(inner_ref.shape[0] - EDGE, EDGE)
    copies = [
        pltpu.make_async_copy(inner_ref.at[last, :], out_ref.at[:, :width], sems.at[0]),
        pltpu.make_async_copy(proj_ref.at[last, :], out_ref.at[:, width:], sems.at[1]),
        first_chunk(inner_ref, head_ref, sems.at[2], 0),
    ]
    for copy in copies:
        copy.start()
    for copy in copies:
        copy.wait()


def last_rows(inner, proj):
    width = inner.shape[1] + proj.shape[1]
    return pl.pallas_call(
        edges_kernel,
        in_specs=[anywhere()] * 2,
        out_specs=[vmem()] * 2,
        out_shape=[jax.ShapeDtypeStruct((EDGE, width), BF16), jax.ShapeDtypeStruct((CHUNK, inner.shape[1] // GROUPS), BF16)],
        scratch_shapes=[pltpu.SemaphoreType.DMA((3,))],
        compiler_params=params(),
        name="edges",
    )(inner, proj)


def decay_kernel(decay_ref, step_ref, skip_ref, fwd_ref, inv_ref, dev_ref, fac_ref):
    heads, rows = decay_ref.shape
    chunks = rows // CHUNK
    lower = jnp.where(iota((CHUNK, CHUNK), 0) >= iota((CHUNK, CHUNK), 1), 1.0, 0.0).astype(BF16)
    same = jnp.where(iota((CHUNK, CHUNK), 0) == iota((CHUNK, CHUNK), 1), 1.0, 0.0).astype(BF16)
    copies = LANES // heads
    cums, steps = [], []
    for c in range(chunks):
        at = pl.ds(c * CHUNK, CHUNK)
        decay = jnp.concatenate([decay_ref[:, at]] * copies, axis=0)
        step = jnp.concatenate([step_ref[:, at]] * copies, axis=0)
        cums.append(sum(dot_rows(lower, piece) for piece in pieces(decay, 3)))
        steps.append(sum(dot_rows(same, piece) for piece in pieces(step, 3)))
    totals = [cum[CHUNK - 1 :] for cum in cums]
    middles = [cum[CHUNK // 2 - 1 : CHUNK // 2] for cum in cums]
    before = [jnp.zeros_like(totals[0])]
    for c in range(chunks):
        before.append(before[c] + totals[c])
    fac_ref[...] = jnp.zeros_like(fac_ref)
    for c in range(chunks):
        at = pl.ds(c * CHUNK, CHUNK)
        fwd_ref[at, :] = jnp.exp(cums[c] - middles[c])
        inv_ref[at, :] = jnp.exp(middles[c] - cums[c]) * steps[c]
        dev_ref[at, :] = jnp.exp(before[c] + cums[c])
        following = middles[c + 1] if c + 1 < chunks else 0.0
        fac_ref[c : c + 1, :] = jnp.exp(totals[c] - middles[c] + following)
    fac_ref[chunks : chunks + 1, :] = skip_ref[:1]
    fac_ref[8:9, :] = jnp.exp(before[chunks])


def decays(decay_log, step_size, skip_weight):
    rows, heads = decay_log.shape
    wide = jax.ShapeDtypeStruct((rows, LANES), F32)
    return pl.pallas_call(
        decay_kernel,
        out_shape=(wide, wide, wide, jax.ShapeDtypeStruct((16, LANES), F32)),
        compiler_params=params(),
        name="decays",
    )(decay_log.T, step_size.T, jnp.broadcast_to(jnp.tile(skip_weight, LANES // heads)[None], (8, LANES)))


def project(proj_ref, edge_ref, taps_ref, mix_ref, bt_ref, wide_ref):
    rows, width = proj_ref.shape
    state = width // 2
    taps = [0.5 * taps_ref[k : k + 1, :] for k in range(taps_ref.shape[0])]
    causal = iota((CHUNK, CHUNK), 0) >= iota((CHUNK, CHUNK), 1)
    past = edge_ref.shape[0]
    wide_ref[EDGE - past : EDGE, :] = edge_ref[:, edge_ref.shape[1] - width :].astype(F32)
    wide_ref[EDGE:, :] = proj_ref[...].astype(F32)
    for c in range(rows // CHUNK):
        at = pl.ds(c * CHUNK, CHUNK)
        both = silu_conv(lambda k: wide_ref[pl.ds(EDGE + c * CHUNK - k, CHUNK), :], taps).astype(BF16)
        b_rows, c_rows = both[:, :state], both[:, state:]
        mix_ref[at, :CHUNK] = jnp.where(causal, dot_rows(c_rows, b_rows), 0.0).astype(BF16)
        mix_ref[at, CHUNK:] = c_rows
        bt_ref[:, at] = b_rows.astype(F32).T.astype(BF16)


def summarize(place_ref, in_ref, ready, edge_ref, taps_ref, inv_ref, fac_ref, bt_ref, x_ref, scaled_ref, opening_ref, slots, window_ref, sum_ref, row_ref, half_ref, head_width, first):
    rows, wide = x_ref.shape
    cols = wide // SQUARE
    state = bt_ref.shape[0]
    count = taps_ref.shape[0]
    chunks = rows // CHUNK
    for block in range(wide // LANES):
        at_lanes = pl.ds(first + block * LANES, LANES)
        window_ref[block, EDGE + CHUNK - count + 1 :, :] = edge_ref[:, at_lanes].astype(F32)
        half_ref[block] = 0.5 * taps_ref[:, at_lanes]
    row_ref[...] = over_heads(fac_ref[...], head_width, first, wide)
    sum_ref[...] = jnp.zeros_like(sum_ref)

    def chunk_step(c, _):
        ready(c)
        at = pl.ds(pl.multiple_of(c * CHUNK, CHUNK), CHUNK)
        for sub in range(wide // SUB):
            at_cols = pl.ds(sub * SUB, SUB)
            here = first + sub * SUB
            rows_here = in_ref[at, at_cols].astype(F32)
            xs = []
            for lane in range(0, SUB, LANES):
                block = (sub * SUB + lane) // LANES
                window_ref[block, EDGE - 8 : EDGE, :] = window_ref[block, EDGE + CHUNK - 8 :, :]
                window_ref[block, EDGE:, :] = rows_here[:, lane : lane + LANES]
                taps = [half_ref[block, k : k + 1, :] for k in range(count)]
                xs.append(silu_conv(lambda k: window_ref[block, pl.ds(EDGE - k, CHUNK), :], taps))
            x = jnp.concatenate(xs, axis=1)
            x_ref[at, at_cols] = x.astype(BF16)
            scaled = over_heads(inv_ref[at, :], head_width, here, SUB).astype(BF16) * x.astype(BF16)
            scaled_ref[at, at_cols] = scaled
            running = sum_ref[:, at_cols]
            opening_ref[at, at_cols] = running.astype(BF16)
            sum_ref[:, at_cols] = row_ref[pl.ds(c, 1), at_cols] * (running + dot(bt_ref[:, at], scaled))
        return 0

    lax.fori_loop(0, chunks, chunk_step, 0)
    row = iota((EDGE, cols), 0)
    for k, slot in enumerate(slots):
        start = pl.multiple_of((k ^ lax.rem(place_ref[0], SQUARE)) * cols, cols)
        slot[:state, :] = sum_ref[:, pl.ds(start, cols)].astype(BF16)
        decay = row_ref[8:16, pl.ds(start, cols)][:1]
        high = decay.astype(BF16).astype(F32)
        slot[state:, :] = jnp.where(row == 0, high, jnp.where(row == 1, decay - high, 0.0)).astype(BF16)


def first_kernel(place_ref, in_ref, head_ref, proj_ref, edge_ref, taps_ref, proj_taps_ref, inv_ref, fac_ref, x_ref, scaled_ref, opening_ref, mix_ref, bt_ref, next_ref, *rest, head_width):
    slots, (block_ref, wide_ref, window_ref, sum_ref, row_ref, half_ref, sems) = rest[:SQUARE], rest[SQUARE:]
    rows, wide = x_ref.shape

    def fetch(c):
        at = pl.ds(pl.multiple_of(c * CHUNK, CHUNK), CHUNK)
        return pltpu.make_async_copy(in_ref.at[at, pl.ds(0, wide)], block_ref.at[at, :], sems.at[c])

    for c in range(1, rows // CHUNK):
        fetch(c).start()
    upcoming = first_chunk(in_ref, next_ref, sems.at[0], wide)
    upcoming.start()
    block_ref[:CHUNK, :] = head_ref[...]
    project(proj_ref, edge_ref, proj_taps_ref, mix_ref, bt_ref, wide_ref)
    summarize(place_ref, block_ref, lambda c: pl.when(c > 0)(lambda: fetch(c).wait()), edge_ref, taps_ref, inv_ref, fac_ref, bt_ref, x_ref, scaled_ref, opening_ref, slots, window_ref, sum_ref, row_ref, half_ref, head_width, 0)
    upcoming.wait()


def slot_shapes(state, wide):
    return [jax.ShapeDtypeStruct((state + EDGE, wide // SQUARE), BF16)] * SQUARE


def sum_scratch(state, wide, taps):
    return [pltpu.VMEM((wide // LANES, EDGE + CHUNK, LANES), F32), pltpu.VMEM((state, wide), F32), pltpu.VMEM((16, wide), F32), pltpu.VMEM((wide // LANES, taps, LANES), F32)]


def first_states(place, inner, head, proj, edge, taps, proj_taps, inv, fac, head_width):
    rows, width = inner.shape
    state = proj.shape[1] // 2
    wide = width // GROUPS
    chunks = rows // CHUNK
    out = pl.pallas_call(
        lambda *refs: first_kernel(*refs, head_width=head_width),
        in_specs=[smem(), anywhere()] + [vmem()] * 7,
        out_specs=[vmem()] * (SQUARE + 6),
        out_shape=[
            jax.ShapeDtypeStruct((rows, wide), BF16),
            jax.ShapeDtypeStruct((rows, wide), BF16),
            jax.ShapeDtypeStruct((chunks * state, wide), BF16),
            jax.ShapeDtypeStruct((rows, CHUNK + state), BF16),
            jax.ShapeDtypeStruct((state, rows), BF16),
            jax.ShapeDtypeStruct((CHUNK, wide), BF16),
        ]
        + slot_shapes(state, wide),
        scratch_shapes=[pltpu.VMEM((rows, wide), BF16), pltpu.VMEM((EDGE + rows, 2 * state), F32)]
        + sum_scratch(state, wide, taps.shape[0])
        + [pltpu.SemaphoreType.DMA((chunks,))],
        compiler_params=params(),
        name="first_states",
    )(place, inner, head, proj, edge, taps, proj_taps, inv, fac)
    return out[:3], out[3:6], out[6:]


def later_kernel(place_ref, in_ref, head_ref, edge_ref, taps_ref, inv_ref, fac_ref, bt_ref, x_ref, scaled_ref, opening_ref, *rest, head_width, first):
    slots, (block_ref, window_ref, sum_ref, row_ref, half_ref, sems) = rest[:SQUARE], rest[SQUARE:]
    rows, wide = x_ref.shape

    def fetch(c):
        at = pl.ds(pl.multiple_of(c * CHUNK, CHUNK), CHUNK)
        return pltpu.make_async_copy(in_ref.at[at, pl.ds(first, wide)], block_ref.at[at, :], sems.at[c])

    for c in range(1, rows // CHUNK):
        fetch(c).start()
    block_ref[:CHUNK, :] = head_ref[...]
    summarize(place_ref, block_ref, lambda c: pl.when(c > 0)(lambda: fetch(c).wait()), edge_ref, taps_ref, inv_ref, fac_ref, bt_ref, x_ref, scaled_ref, opening_ref, slots, window_ref, sum_ref, row_ref, half_ref, head_width, first)


def later_states(place, inner, head, edge, taps, inv, fac, bt, head_width, group):
    rows, width = inner.shape
    wide = width // GROUPS
    state = bt.shape[0]
    chunks = rows // CHUNK
    out = pl.pallas_call(
        lambda *refs: later_kernel(*refs, head_width=head_width, first=group * wide),
        in_specs=[smem(), anywhere()] + [vmem()] * 6,
        out_specs=[vmem()] * (SQUARE + 3),
        out_shape=[
            jax.ShapeDtypeStruct((rows, wide), BF16),
            jax.ShapeDtypeStruct((rows, wide), BF16),
            jax.ShapeDtypeStruct((chunks * state, wide), BF16),
        ]
        + slot_shapes(state, wide),
        scratch_shapes=[pltpu.VMEM((rows, wide), BF16)] + sum_scratch(state, wide, taps.shape[0]) + [pltpu.SemaphoreType.DMA((chunks,))],
        compiler_params=params(),
        name="later_states",
    )(place, inner, head, edge, taps, inv, fac, bt)
    return out[:3], out[3:]


def combine_kernel(place_ref, *refs):
    slots, (leaving_ref, prefix_ref, opening_ref, placed_ref) = refs[:SQUARE], refs[SQUARE:]
    state, cols = leaving_ref.shape
    spot = lax.rem(place_ref[0], SQUARE)
    for k in range(SQUARE):
        placed_ref[spot ^ k] = slots[k][...]
    running = jnp.zeros((state, cols), F32)
    opening = jnp.ones((1, cols), F32)
    begun = jnp.where(place_ref[0] < SQUARE, 0.0, 1.0)
    for p in range(SQUARE):
        prefix_ref[spot ^ p] = running
        opening_ref[spot ^ p] = jnp.broadcast_to(begun * opening, (8, cols))
        tail = placed_ref[p, state:, :].astype(F32)
        decay = tail[0:1] + tail[1:2]
        running = decay * running + placed_ref[p, :state, :].astype(F32)
        opening = decay * opening
    leaving_ref[...] = running.astype(BF16)
    opening_ref[SQUARE] = jnp.broadcast_to(opening, (8, cols))


def combine(place, slots):
    rows, cols = slots[0].shape
    state = rows - EDGE
    return pl.pallas_call(
        combine_kernel,
        in_specs=[smem()] + [vmem()] * SQUARE,
        out_specs=[vmem()] * 3,
        out_shape=(
            jax.ShapeDtypeStruct((state, cols), BF16),
            jax.ShapeDtypeStruct((SQUARE, state, cols), F32),
            jax.ShapeDtypeStruct((SQUARE + 1, 8, cols), F32),
        ),
        scratch_shapes=[pltpu.VMEM((SQUARE, rows, cols), BF16)],
        compiler_params=params(),
        name="combine",
    )(place, *slots)


def local_kernel(x_ref, scaled_ref, opening_ref, fwd_ref, fac_ref, mix_ref, out_ref, *, head_width, first):
    rows, wide = x_ref.shape
    chunks = rows // CHUNK
    state = opening_ref.shape[0] // chunks
    cols = wide // SQUARE

    def tile_step(j, _):
        base = pl.multiple_of(j * cols, cols)
        at_cols = pl.ds(base, cols)
        skip = over_heads(fac_ref[...], head_width, first + base, cols)[chunks : chunks + 1]
        for c in range(chunks):
            at = pl.ds(c * CHUNK, CHUNK)
            both = jnp.concatenate([scaled_ref[at, at_cols], opening_ref[pl.ds(c * state, state), at_cols]], axis=0)
            mixed = over_heads(fwd_ref[at, :], head_width, first + base, cols) * dot(mix_ref[at, :], both)
            out_ref[at, at_cols] = mixed + skip * x_ref[at, at_cols].astype(F32)
        return 0

    lax.fori_loop(0, SQUARE, tile_step, 0, unroll=2)


def local_parts(x, scaled, opening, fwd, fac, mix, head_width, group):
    rows, wide = x.shape
    return pl.pallas_call(
        lambda *refs: local_kernel(*refs, head_width=head_width, first=group * wide),
        in_specs=[vmem()] * 6,
        out_specs=vmem(),
        out_shape=jax.ShapeDtypeStruct((rows, wide), F32),
        compiler_params=params(),
        name="local",
    )(x, scaled, opening, fwd, fac, mix)


def normalize(place_ref, local_ref, dev_ref, mix_ref, gain_ref, slots, head_width, first, done):
    rows, wide = local_ref.shape
    cols = wide // SQUARE
    mean = jnp.where(iota((SUB, SUB), 0) // head_width == iota((SUB, SUB), 1) // head_width, 1.0 / head_width, 0.0).astype(BF16)
    for k in range(SQUARE):
        base = pl.multiple_of((k ^ lax.rem(place_ref[0], SQUARE)) * cols, cols)
        for sub in range(cols // SUB):
            at_cols = pl.ds(base + sub * SUB, SUB)
            here = first + base + sub * SUB
            carried = dot(mix_ref[:, CHUNK:], slots[k][:, sub * SUB : (sub + 1) * SUB])
            combined = local_ref[:, at_cols] + over_heads(dev_ref[...], head_width, here, SUB) * carried
            squares = dot((combined * combined).astype(BF16), mean)
            result = combined * lax.rsqrt(squares + 1e-05) * gain_ref[:, pl.ds(here, SUB)]
            done(k * (cols // SUB) + sub, base + sub * SUB, result.astype(BF16))


def finish_first_kernel(place_ref, local_ref, dev_ref, mix_ref, gain_ref, *rest, head_width):
    slots, out_ref = rest[:SQUARE], rest[SQUARE]

    def done(turn, column, result):
        out_ref[:, pl.ds(column, SUB)] = result

    normalize(place_ref, local_ref, dev_ref, mix_ref, gain_ref, slots, head_width, 0, done)


def finish_first(place, local, dev, mix, gain, slots, head_width):
    rows, wide = local.shape
    return pl.pallas_call(
        lambda *refs: finish_first_kernel(*refs, head_width=head_width),
        in_specs=[smem()] + [vmem()] * (4 + SQUARE),
        out_specs=vmem(),
        out_shape=jax.ShapeDtypeStruct((rows, wide), BF16),
        compiler_params=params(),
        name="finish_first",
    )(place, local, dev, mix, gain, *slots)


def finish_kernel(place_ref, local_ref, dev_ref, mix_ref, gain_ref, *rest, head_width):
    slots, (earlier_ref, out_ref, stage_ref, sems, earlier_sem) = rest[:SQUARE], rest[SQUARE:]
    first = earlier_ref.shape[1]
    earlier = pltpu.make_async_copy(earlier_ref, out_ref.at[:, pl.ds(0, first)], earlier_sem)
    earlier.start()
    copies = []

    def done(turn, column, result):
        stage_ref[turn] = result
        copies.append(pltpu.make_async_copy(stage_ref.at[turn], out_ref.at[:, pl.ds(first + column, SUB)], sems.at[turn]))
        copies[-1].start()

    normalize(place_ref, local_ref, dev_ref, mix_ref, gain_ref, slots, head_width, first, done)
    earlier.wait()
    for copy in copies:
        copy.wait()


def finish(place, local, dev, mix, gain, slots, earlier, head_width):
    rows, wide = local.shape
    return pl.pallas_call(
        lambda *refs: finish_kernel(*refs, head_width=head_width),
        in_specs=[smem()] + [vmem()] * (5 + SQUARE),
        out_specs=anywhere(),
        out_shape=jax.ShapeDtypeStruct((rows, wide * GROUPS), BF16),
        scratch_shapes=[pltpu.VMEM((wide // SUB, rows, SUB), BF16), pltpu.SemaphoreType.DMA((wide // SUB,)), pltpu.SemaphoreType.DMA],
        compiler_params=params(),
        name="finish",
    )(place, local, dev, mix, gain, *slots, earlier)


def shifted(x, by):
    length = lax.axis_size("ctx")
    return lax.ppermute(x, "ctx", [(i, i + by) for i in range(length - by)])


def swapped(x, k):
    length = lax.axis_size("ctx")
    return lax.ppermute(x, "ctx", [(i, i ^ k) for i in range(length)])


def exchanged(slots):
    received = [swapped(slots[k], k) for k in range(SQUARE - 1, 0, -1)]
    return [slots[0]] + received[::-1]


def previous_squares(leaving, decay):
    length = lax.axis_size("ctx")
    squares = length // SQUARE
    entering = lax.ppermute(leaving, "ctx", [(i, (i + SQUARE) % length) for i in range(length)])
    span = 1
    if squares > 2:
        entering = jnp.where(lax.axis_index("ctx") < SQUARE, jnp.zeros_like(entering), entering)
        window = shifted(decay, SQUARE)
    while span < squares - 1:
        behind = shifted(entering, SQUARE * span)
        entering = (entering.astype(F32) + window * behind.astype(F32)).astype(BF16)
        window = window * shifted(window, SQUARE * span)
        span *= 2
    return entering


def body(inner_input, state_proj, step_size, decay_log, conv_inner, conv_proj, skip_weight, norm_gain):
    rows, width = inner_input.shape
    heads = step_size.shape[1]
    head_width = width // heads
    past = conv_inner.shape[0] - 1
    kept, kept_proj = [pltpu.with_memory_space_constraint(a, pltpu.HBM) for a in (inner_input, state_proj)]
    place = jnp.full((1,), lax.axis_index("ctx"), jnp.int32)
    edge, head = last_rows(kept, kept_proj)
    edge = shifted(edge[EDGE - past :], 1)
    fwd, inv, dev, fac = decays(decay_log, step_size, skip_weight)
    gain = norm_gain[None]
    made, sent = [], []
    parts, (mix, bt, head), slots = first_states(place, kept, head, state_proj, edge, conv_inner, conv_proj, inv, fac, head_width)
    made.append(parts)
    sent.append(exchanged(slots))
    parts, slots = later_states(place, kept, head, edge, conv_inner, inv, fac, bt, head_width, 1)
    made.append(parts)
    sent.append(exchanged(slots))
    made[0], sent[0] = lax.optimization_barrier((made[0], sent[0]))
    combined = [combine(place, sent[0])]
    locals_ = [local_parts(*made[group], fwd, fac, mix, head_width, group) for group in range(GROUPS)]
    sent[1], locals_[0] = lax.optimization_barrier((sent[1], locals_[0]))
    combined.append(combine(place, sent[1]))
    arrived = [previous_squares(leaving, opening[SQUARE, :1]) for leaving, _, opening in combined]
    arrived[1], locals_[1] = lax.optimization_barrier((arrived[1], locals_[1]))
    returned = []
    for group in range(GROUPS):
        _, prefix, opening = combined[group]
        entering = [(prefix[k] + opening[k, :1] * arrived[group].astype(F32)).astype(BF16) for k in range(SQUARE)]
        returned.append(exchanged(entering))
    earlier = finish_first(place, locals_[0], dev, mix, gain, returned[0], head_width)
    return finish(place, locals_[1], dev, mix, gain, returned[1], earlier, head_width)


def solution(mesh):
    split = P(("dp", "ctx"), None)
    return jax.shard_map(
        body, mesh=mesh, in_specs=(split, split, split, split, P(), P(), P(), P()), out_specs=split, check_vma=False
    )
```
